128 devices in a mesh: gx: 8 (over z, core), gy: 16 (over y, x).
Axes of the slice: x: 4, y: 4, z: 4, core: 2. Of those that a mesh axis runs over, the one named last changes fastest.
Arguments:
- seg_source: float32 [9, 64, 2048], P(None, 'gx', 'gy'), may hold values from -0.3125 to 0.3125
- seg_inverse: float32 [9, 9, 64, 2048], P(None, None, 'gx', 'gy')
- seg_outflow: float32 [9, 9, 64, 2048], P(None, None, 'gx', 'gy')
- well_len: int32 [64], P('gx'), may hold values from 1 to 2048, as said below
- perf_seg: int32 [8, 16, 16, 256], P('gx', 'gy'), may hold values from 0 to 1023, as said below
- perf_count: int32 [8, 16, 16], P('gx', 'gy'), may hold values from 0 to 256, as said below
- perf_coupling: float32 [9, 9, 8, 16, 16, 256], P(None, None, 'gx', 'gy'), may hold values from -3 to 3
- recv_cell: int32 [8, 16, 16, 256], P('gx', 'gy'), may hold values from 0 to 8191
- cell_cot: bfloat16 [9, 64, 128, 128], P(None, 'gx', 'gy'), may hold values from -6 to 6
- start_iterate: float32 [9, 64, 128, 128], P(None, 'gx', 'gy'), may hold values from -6 to 6
- accumulation: bfloat16 [9, 64, 128, 128], P(None, 'gx', 'gy'), may hold values from 0.049804688 to 0.5
- mobility: bfloat16 [9, 64, 128, 128], P(None, 'gx', 'gy'), may hold values from 0.19921875 to 2
- perm_x: float32 [64, 128, 128], P('gx', 'gy'), may hold values from 0.3 to 1.5
- perm_y: float32 [64, 128, 128], P('gx', 'gy'), may hold values from 0.3 to 1.5
- perm_z: float32 [64, 128, 128], P('gx', 'gy'), may hold values from 0.3 to 1.5
Outputs:
- seg_adjoint: float32 [9, 64, 2048], P(None, 'gx', 'gy')
- cell_adjoint: float32 [9, 64, 128, 128], P(None, 'gx', 'gy')
The draws below stay inside these ranges and needn't reach their ends.
Inputs may be any that keep to these rules, and one draw needn't show every extreme that they name: perf_count[i, j, b] is 0 where |b - j| > 8 and equals 256 where b = j. `well_len`: every index of gx has a well of 2048 active segments. `perf_seg`: every row names a segment slot q of brick (i, j) whose segment is active: j * 128 + q % 128 < well_len[i * 8 + q // 128].
All inputs are finite; a program needn't handle non-finite values.
Results may differ from the reference program's by a relative error of at most 0.00035.
Values sent between devices are 32-bit elements; how exact they have to be, the bound alone decides.
No kernel may reach another device: no remote copies, remote signals or barrier semaphores. Data moves between devices by JAX's collectives and lax.ppermute only.
A program may use at most 128 MiB of HBM per device.

```python
import math
import jax
import jax.numpy as jnp
from jax import lax

NC = 9
BX = 8
BY = 8
LZ = 128
W_G = 8
SP = 128
CAP = 256
SWEEPS = 6
WELL_PIECE_CAP = 2048
NWELLS = 64
NX = 64
NY = 128
N_GX = 8
N_GY = 16


def well_blocks(key):
    divide_seeds = [jax.random.fold_in(key, 101 + index) for index in range(6)]
    tile_span = (NC, NWELLS, WELL_PIECE_CAP)
    spread = 0.2 / WELL_PIECE_CAP ** 0.5
    identity = jnp.eye(NC, dtype=jnp.float32)[:, :, None, None]
    scale_diag = jax.random.uniform(divide_seeds[0], tile_span, jnp.float32, 0.9, 1.1)
    off_inverse = spread * jax.random.normal(divide_seeds[1], (NC, NC, NWELLS, WELL_PIECE_CAP), jnp.float32) * (1.0 - identity)
    inverse = identity * scale_diag[None] + off_inverse
    low_log = jnp.log(30.0)
    falloff_scale = jnp.exp(jax.random.uniform(divide_seeds[2], (NC, NWELLS, 1), jnp.float32, low_log, jnp.log(8.0 * WELL_PIECE_CAP)))
    jitter_shift = jax.random.uniform(divide_seeds[3], tile_span, jnp.float32, 0.5, 1.5)
    spike_layout = jnp.where(jax.random.bernoulli(divide_seeds[4], 2.0 / WELL_PIECE_CAP, tile_span), 0.7, 1.0)
    keep_share = jnp.exp(-jitter_shift / falloff_scale) * spike_layout
    off_outflow = spread * jax.random.normal(divide_seeds[5], (NC, NC, NWELLS, WELL_PIECE_CAP), jnp.float32) * (1.0 - identity)
    outflow = -identity * (keep_share / scale_diag)[None] + off_outflow
    return (inverse, outflow)


def draw_seg_inverse(key, part):
    return well_blocks(key)[0]


def draw_seg_outflow(key, part):
    return well_blocks(key)[1]


def draw_well_len(key, part):
    uniform_len = jax.random.randint(jax.random.fold_in(key, 7), (NWELLS,), 1, WELL_PIECE_CAP + 1)
    cubed = jnp.maximum(uniform_len * uniform_len // WELL_PIECE_CAP * uniform_len // WELL_PIECE_CAP, 1)
    row_count = NWELLS // W_G
    chosen = jnp.arange(row_count) * W_G + jax.random.randint(jax.random.fold_in(key, 8), (row_count,), 0, W_G)
    return cubed.at[chosen].set(WELL_PIECE_CAP).astype(jnp.int32)


def draw_perf_seg(key, part):
    row_count = NWELLS // W_G
    groups = WELL_PIECE_CAP // SP
    lens = draw_well_len(key, part).reshape(row_count, W_G)
    brick_start = (jnp.arange(groups, dtype=jnp.int32) * SP)[None, None, :]
    reach = jnp.clip(lens[:, :, None] - brick_start, 0, SP)
    full_well = jnp.argmax((lens == WELL_PIECE_CAP).astype(jnp.int32), axis=1).astype(jnp.int32)
    shape = (row_count, groups, groups, CAP)
    picked_well = jax.random.randint(jax.random.fold_in(key, 21), shape, 0, W_G)
    reach_t = jnp.transpose(reach, (0, 2, 1))
    flat_reach = reach_t.reshape(row_count, groups, W_G, 1)
    gather_idx = picked_well.reshape(row_count, groups, groups * CAP, 1)
    gather_idx = jnp.transpose(gather_idx, (0, 1, 3, 2)).reshape(row_count, groups, 1, groups * CAP)
    got = jnp.take_along_axis(jnp.broadcast_to(flat_reach, (row_count, groups, W_G, groups * CAP)), jnp.broadcast_to(gather_idx, (row_count, groups, 1, groups * CAP)), axis=2)
    got = got.reshape(shape)
    use_full = got == 0
    well_final = jnp.where(use_full, full_well[:, None, None, None], picked_well)
    count_final = jnp.where(use_full, SP, got)
    slot = jax.random.randint(jax.random.fold_in(key, 22), shape, 0, jnp.maximum(count_final, 1))
    return (well_final * SP + slot).astype(jnp.int32)


def draw_perf_count(key, part):
    groups = WELL_PIECE_CAP // SP
    row_count = NWELLS // W_G
    base_count = jax.random.randint(jax.random.fold_in(key, 9), (row_count, groups, groups), CAP // 2, CAP + 1)
    src_brick = jnp.arange(groups)[None, :, None]
    dst_brick = jnp.arange(groups)[None, None, :]
    gap_bricks = jnp.abs(dst_brick - src_brick)
    counts = jnp.where(gap_bricks <= groups // 2, base_count // (1 + gap_bricks // 4), 0)
    counts = jnp.where(gap_bricks == 0, CAP, counts)
    return counts.astype(jnp.int32)


def with_ends(array, rng, low, largest):
    longest = array.shape.index(max(array.shape))
    spots = []
    for shift in (0, 1):
        where = [jax.random.randint(jax.random.fold_in(rng, axis), (), 0, length) for axis, length in enumerate(array.shape)]
        where[longest] = (where[longest] + shift) % array.shape[longest]
        spots.append(tuple(where))
    return array.at[spots[0]].set(low).at[spots[1]].set(largest)


def levels(rng, extent, split, low, largest):
    factor_of, own = 1.0, jax.random.fold_in(rng, 6)
    for axis_at, blocks in split:
        steps = jnp.exp(jax.random.uniform(jax.random.fold_in(own, axis_at), (blocks,), jnp.float32, low / len(split), largest / len(split)))
        factor_of = factor_of * jnp.repeat(steps, extent[axis_at] // blocks).reshape([-1 if axis == axis_at else 1 for axis in range(len(extent))])
    return factor_of


def centred(rng, shape, scale, most, cuts=(), kind=jnp.bfloat16):
    loudness = levels(rng, shape, cuts, -0.22, 0.18) if cuts else 1.0
    drawn = jax.random.normal(rng, shape, jnp.float32) * scale * loudness
    return jnp.minimum(jnp.maximum(drawn, -most), most).astype(kind)


def setup_inputs(seed: int = 0) -> dict:
    key_of = jax.random.split(jax.random.key(seed), 16)
    seg_source = centred(key_of[0], (NC, NWELLS, WELL_PIECE_CAP), (1.0 / WELL_PIECE_CAP ** 0.5), 0.3125, ((1, 8), (2, 16)), jnp.float32)
    seg_inverse = draw_seg_inverse(jax.random.fold_in(key_of[15], 71), 0)
    seg_outflow = draw_seg_outflow(jax.random.fold_in(key_of[15], 71), 0)
    well_len = draw_well_len(jax.random.fold_in(key_of[15], 71), 0)
    perf_seg = draw_perf_seg(jax.random.fold_in(key_of[15], 71), 0)
    perf_count = draw_perf_count(jax.random.fold_in(key_of[15], 71), 0)
    perf_coupling = centred(key_of[6], (NC, NC, N_GX, N_GY, N_GY, CAP), 0.5, 3.0, ((2, 8), (3, 16)), jnp.float32)
    recv_cell = with_ends(jax.random.randint(key_of[7], (N_GX, N_GY, N_GY, CAP), 0, BX * BY * LZ), jax.random.fold_in(key_of[7], 1), 0, (BX * BY * LZ) - 1).astype(jnp.int32)
    cell_cot = centred(key_of[8], (NC, NX, NY, LZ), 1.0, 6.0, ((1, 8), (2, 16)))
    start_iterate = centred(key_of[9], (NC, NX, NY, LZ), 1.0, 6.0, ((1, 8), (2, 16)), jnp.float32)
    accumulation = jnp.clip(jnp.exp(math.log(0.5) - 2.306499 * jax.random.uniform(key_of[10], (NC, NX, NY, LZ), jnp.float32) ** levels(key_of[10], (NC, NX, NY, LZ), ((1, 8), (2, 16)), -0.2, 0.2)), 0.049804688, 0.5).astype(jnp.bfloat16)
    mobility = jnp.clip(jnp.exp(math.log(2.0) - 2.306499 * jax.random.uniform(key_of[11], (NC, NX, NY, LZ), jnp.float32) ** levels(key_of[11], (NC, NX, NY, LZ), ((1, 8), (2, 16)), -0.2, 0.2)), 0.19921875, 2.0).astype(jnp.bfloat16)
    perm_x = jnp.clip(jnp.exp(math.log(1.5) - 1.60943787 * jax.random.uniform(key_of[12], (NX, NY, LZ), jnp.float32) ** levels(key_of[12], (NX, NY, LZ), ((0, 8), (1, 16)), -0.2, 0.2)), 0.3, 1.5)
    perm_y = jnp.clip(jnp.exp(math.log(1.5) - 1.60943787 * jax.random.uniform(key_of[13], (NX, NY, LZ), jnp.float32) ** levels(key_of[13], (NX, NY, LZ), ((0, 8), (1, 16)), -0.2, 0.2)), 0.3, 1.5)
    perm_z = jnp.clip(jnp.exp(math.log(1.5) - 1.60943787 * jax.random.uniform(key_of[14], (NX, NY, LZ), jnp.float32) ** levels(key_of[14], (NX, NY, LZ), ((0, 8), (1, 16)), -0.2, 0.2)), 0.3, 1.5)
    return dict(seg_source=seg_source, seg_inverse=seg_inverse, seg_outflow=seg_outflow, well_len=well_len, perf_seg=perf_seg, perf_count=perf_count, perf_coupling=perf_coupling, recv_cell=recv_cell, cell_cot=cell_cot, start_iterate=start_iterate, accumulation=accumulation, mobility=mobility, perm_x=perm_x, perm_y=perm_y, perm_z=perm_z)


OMEGA = 0.8
PRECISE = lax.Precision.HIGHEST


def relax(iterate, perm_wide_x, perm_wide_y, perm_mid_z, accum_cells, mobil_cells, source, inside):
    centre_x = perm_wide_x[1:-1, 1:-1]
    t_east = centre_x * perm_wide_x[2:, 1:-1]
    t_west = centre_x * perm_wide_x[:-2, 1:-1]
    centre_y = perm_wide_y[1:-1, 1:-1]
    t_north = centre_y * perm_wide_y[1:-1, 2:]
    t_south = centre_y * perm_wide_y[1:-1, :-2]
    flat_zero = jnp.zeros_like(perm_mid_z[..., :1])
    t_up = jnp.concatenate([perm_mid_z[..., :-1] * perm_mid_z[..., 1:], flat_zero], axis=-1)
    t_down = jnp.concatenate([flat_zero, perm_mid_z[..., 1:] * perm_mid_z[..., :-1]], axis=-1)
    middle = iterate[:, 1:-1, 1:-1]
    level_zero = jnp.zeros_like(middle[..., :1])
    above = jnp.concatenate([middle[..., 1:], level_zero], axis=-1)
    below = jnp.concatenate([level_zero, middle[..., :-1]], axis=-1)
    total = t_east + t_west + t_north + t_south + t_up + t_down
    beside = t_east * iterate[:, 2:, 1:-1] + t_west * iterate[:, :-2, 1:-1]
    beside = beside + t_north * iterate[:, 1:-1, 2:] + t_south * iterate[:, 1:-1, :-2]
    beside = beside + t_up * above + t_down * below
    applied = accum_cells * middle + mobil_cells * (total * middle - beside)
    diagonal = accum_cells + mobil_cells * total
    return middle + inside * OMEGA * (source - applied) / (diagonal + 1.0 - inside)


def reference(seg_source, seg_inverse, seg_outflow, well_len, perf_seg, perf_count, perf_coupling, recv_cell, cell_cot, start_iterate, accumulation, mobility, perm_x, perm_y, perm_z):
    active = (jnp.arange(WELL_PIECE_CAP).astype(jnp.int32)[None, :] < well_len[:, None]).astype(jnp.float32)
    inverse_lead = jnp.moveaxis(seg_inverse, 3, 0)
    outflow_lead = jnp.moveaxis(seg_outflow, 3, 0)
    source_lead = jnp.moveaxis(seg_source, 2, 0)
    active_lead = active.T

    def backward_step(after_lam, blocks):
        inverse_blk, outflow_blk, source_blk, active_blk = blocks
        pushed = source_blk - jnp.einsum("kjw,kw->jw", outflow_blk, after_lam, precision=PRECISE)
        lam_now = active_blk[None, :] * jnp.einsum("jcw,jw->cw", inverse_blk, pushed, precision=PRECISE)
        return lam_now, lam_now

    start_lam = jnp.zeros((NC, NWELLS), jnp.float32)
    _, lam_all = lax.scan(backward_step, start_lam, (inverse_lead, outflow_lead, source_lead, active_lead), reverse=True)
    seg_adjoint = jnp.moveaxis(lam_all, 0, 2)

    row_index = jnp.arange(N_GX).astype(jnp.int32)[:, None, None, None]
    col_index = jnp.arange(N_GY).astype(jnp.int32)[None, :, None, None]
    dst_index = jnp.arange(N_GY).astype(jnp.int32)[None, None, :, None]
    well_index = row_index * W_G + perf_seg // SP
    seg_index = col_index * SP + perf_seg % SP
    picked = seg_adjoint[:, well_index, seg_index]
    live_rows = (jnp.arange(CAP).astype(jnp.int32)[None, None, None, :] < perf_count[..., None]).astype(jnp.float32)
    sent_rows = live_rows[None] * jnp.einsum("kcijbp,kijbp->cijbp", perf_coupling, picked, precision=PRECISE)
    recv_sender = jnp.transpose(recv_cell, (0, 2, 1, 3))
    cell_x = row_index * BX + recv_sender // (BY * LZ)
    cell_y = dst_index * BY + (recv_sender // LZ) % BY
    cell_z = recv_sender % LZ
    flat_index = ((cell_x * NY + cell_y) * LZ + cell_z).reshape(-1)
    well_part = jnp.zeros((NC, NX * NY * LZ), jnp.float32).at[:, flat_index].add(sent_rows.reshape(NC, -1))
    source = cell_cot.astype(jnp.float32) - well_part.reshape(NC, NX, NY, LZ)

    perm_pad_x = jnp.pad(perm_x, ((1, 1), (1, 1), (0, 0)))
    perm_pad_y = jnp.pad(perm_y, ((1, 1), (1, 1), (0, 0)))

    def solve_one(component):
        comp_source, comp_iter, comp_acc, comp_mob = component
        for sweep in range(SWEEPS):
            padded = jnp.pad(comp_iter[None], ((0, 0), (1, 1), (1, 1), (0, 0)))
            comp_iter = relax(padded, perm_pad_x, perm_pad_y, perm_z, comp_acc[None], comp_mob[None], comp_source[None], 1.0)[0]
        return comp_iter

    cell_adjoint = lax.map(solve_one, (source, start_iterate, accumulation.astype(jnp.float32), mobility.astype(jnp.float32)))
    return seg_adjoint, cell_adjoint
```

```python
import jax
import jax.numpy as jnp
from jax import lax
from jax.experimental import pallas as pl
from jax.experimental.pallas import tpu as pltpu
from jax.sharding import PartitionSpec as P

F32 = jnp.float32
BF16 = jnp.bfloat16
I32 = jnp.int32
NC = 9
OMEGA = 0.8
KEEP = 1.0 - OMEGA
BRICKS = 16
EARLY = 6
LATE = 5
TILE = (8, 128)
FIELDS = 21
EARLY_ROWS = 16 + FIELDS * 8 * EARLY
LATE_ROWS = 16 + NC * 8 * LATE
RATIO_AT = 12 * EARLY * 24
WIDE_ROWS = RATIO_AT + NC * LATE * 16
COLS = 8 + 2 * LATE
SLOT = 24

VMEM = pl.BlockSpec(memory_space=pltpu.VMEM)
SMEM = pl.BlockSpec(memory_space=pltpu.SMEM)


def lanes_of(shape=TILE):
    return lax.broadcasted_iota(I32, shape, 1)


def rows_of(shape=TILE):
    return lax.broadcasted_iota(I32, shape, 0)


def call(kernel, outs, scratch, specs, name, flops=1_000_000, limit=16):
    return pl.pallas_call(
        kernel,
        out_shape=outs,
        in_specs=specs,
        out_specs=jax.tree.map(lambda _: VMEM, outs),
        scratch_shapes=scratch,
        compiler_params=pltpu.CompilerParams(vmem_limit_bytes=limit * 1024 * 1024),
        cost_estimate=pl.CostEstimate(
            flops=flops, bytes_accessed=1_000_000, transcendentals=0
        ),
        name=name,
    )


def out(*shape):
    return jax.ShapeDtypeStruct(shape, F32)


def scan_kernel(len_ref, src, inv, outf, mats, vecs, head, rolled):
    lane = lanes_of()
    well = rows_of()
    length = jnp.zeros(TILE, I32)
    for w in range(8):
        length = jnp.where(well == w, len_ref[w], length)
    active = (lax.axis_index("gy") * 128 + lane < length).astype(F32)

    def start(c, _):
        row = [inv[j, c] for j in range(NC)]
        total = row[0] * src[0]
        for j in range(1, NC):
            total = total + row[j] * src[j]
        vecs[c] = active * total
        for k in range(NC):
            total = row[0] * outf[k, 0]
            for j in range(1, NC):
                total = total + row[j] * outf[k, j]
            mats[c * NC + k] = -active * total
        return 0

    lax.fori_loop(0, NC, start, 0)

    def step(i, _):
        gap = lax.shift_left(jnp.int32(1), i)
        keep = lane < 128 - gap
        for k in range(NC):
            for m in range(NC):
                moved = pltpu.roll(mats[k * NC + m], 128 - gap, 1)
                rolled[k * 10 + m] = jnp.where(keep, moved, 1.0 if k == m else 0.0)
            rolled[k * 10 + 9] = jnp.where(keep, pltpu.roll(vecs[k], 128 - gap, 1), 0.0)

        def rows(group, _):
            rows3 = [[mats[(group * 3 + a) * NC + k] for k in range(NC)] for a in range(3)]
            for m in range(10):
                right = [rolled[k * 10 + m] for k in range(NC)]
                for a in range(3):
                    total = rows3[a][0] * right[0]
                    for k in range(1, NC):
                        total = total + rows3[a][k] * right[k]
                    if m < NC:
                        mats[(group * 3 + a) * NC + m] = total
                    else:
                        vecs[group * 3 + a] = vecs[group * 3 + a] + total
            return 0

        return lax.fori_loop(0, 3, rows, 0)

    lax.fori_loop(0, 7, step, 0)
    packed = jnp.zeros(TILE, F32)
    for e in range(81):
        moved = mats[e] if e == 0 else pltpu.roll(mats[e], e, 1)
        packed = jnp.where(lane == e, moved, packed)
    for c in range(NC):
        packed = jnp.where(lane == 81 + c, pltpu.roll(vecs[c], 81 + c, 1), packed)
    for j in range(BRICKS):
        head[j] = packed


def rows_kernel(count_ref, mats, vecs, heads, perf_seg, coupling, lam, sent):
    row = rows_of()
    lane = lanes_of()
    me = lax.axis_index("gy")

    def hop(t, incoming):
        head = heads[BRICKS - 1 - t]
        after = []
        for c in range(NC):
            total = jnp.broadcast_to(head[:, 81 + c : 82 + c], TILE)
            for k in range(NC):
                at = c * NC + k
                total = total + jnp.broadcast_to(head[:, at : at + 1], TILE) * incoming[k]
            after.append(total)
        return tuple(after)

    nothing = tuple(jnp.zeros(TILE, F32) for _ in range(NC))
    incoming = lax.fori_loop(0, BRICKS - 1 - me, hop, nothing)
    for c in range(NC):
        total = vecs[c]
        for k in range(NC):
            total = total + mats[c * NC + k] * incoming[k]
        lam[c] = total
    for block in range(2):
        count = jnp.zeros(TILE, I32)
        for b in range(8):
            count = jnp.where(row == b, count_ref[block * 8 + b], count)
        for half in range(2):
            at = (slice(block * 8, block * 8 + 8), slice(half * 128, half * 128 + 128))
            slot = perf_seg[at]
            slot_well = lax.shift_right_logical(slot, 7)
            slot_lane = lax.bitwise_and(slot, 127)
            is_well = [slot_well == w for w in range(8)]
            picked = []
            for k in range(NC):
                total = jnp.zeros(TILE, F32)
                for w in range(8):
                    line = jnp.broadcast_to(lam[k, w : w + 1, :], TILE)
                    got = jnp.take_along_axis(line, slot_lane, axis=1)
                    total = jnp.where(is_well[w], got, total)
                picked.append(total)
            live = lane + half * 128 < count
            for c in range(NC):
                total = coupling[(0, c) + at] * picked[0]
                for k in range(1, NC):
                    total = total + coupling[(k, c) + at] * picked[k]
                total = jnp.where(live, total, 0.0)
                sent[pl.ds(block * 8 * SLOT + c * 2 + half, 8, stride=SLOT), :] = total


def early_pack_kernel(start, px, py, pz, accum, mobil, ratio, send_a, send_b):
    even = lax.rem(lax.axis_index("gy"), 2) == 0
    for i in range(NC * 4):
        at = slice(i * 16, i * 16 + 16)
        ratio[at, :] = accum[at, :].astype(F32) / mobil[at, :].astype(F32)
    for buffer in (send_a, send_b):
        buffer[0:8, :] = jnp.zeros(TILE, F32)
        buffer[EARLY_ROWS - 8 : EARLY_ROWS, :] = jnp.zeros(TILE, F32)
    perms = (px, py, pz)
    for f in range(FIELDS):
        for x in range(8):
            if f < NC:
                low, high = start[f, x, 0:EARLY, :], start[f, x, 8 - EARLY : 8, :]
            elif f < 12:
                low, high = perms[f - 9][x, 0:EARLY, :], perms[f - 9][x, 8 - EARLY : 8, :]
            else:
                base = ((f - 12) * 8 + x) * 8
                low, high = ratio[base : base + EARLY, :], ratio[base + 8 - EARLY : base + 8, :]
            at = 8 + (f * 8 + x) * EARLY
            send_a[at : at + EARLY, :] = jnp.where(even, high, low)
            send_b[at : at + EARLY, :] = jnp.where(even, low, high)


def early_wide_kernel(start, px, py, pz, ratio, recv_a, recv_b, wide, send_a, send_b):
    row = rows_of()
    gy = lax.axis_index("gy")
    even = lax.rem(gy, 2) == 0
    south_in = (gy > 0).astype(F32)
    north_in = (gy < BRICKS - 1).astype(F32)
    perms = (px, py, pz)
    for f in range(FIELDS):
        for x in range(8):
            at = 8 + (f * 8 + x) * EARLY
            low = slice(at - (8 - EARLY), at + EARLY)
            high = slice(at, at + 8)
            south = jnp.where(even, recv_b[low, :], recv_a[low, :])
            north = jnp.where(even, recv_a[high, :], recv_b[high, :])
            if f < NC:
                home = start[f, x]
            elif f < 12:
                home = perms[f - 9][x]
                south = south * south_in
                north = north * north_in
            else:
                base = ((f - 12) * 8 + x) * 8
                home = ratio[base : base + 8, :]
            wide[x, f, 0:8, :] = south
            wide[x, f, 8:16, :] = home
            wide[x, f, 16:24, :] = north
    even_x = lax.rem(lax.axis_index("gx"), 2) == 0
    for buffer, east in ((send_a, even_x), (send_b, jnp.logical_not(even_x))):
        first = jnp.where(east, 8 - EARLY, 0)
        for f in range(12):
            for d in range(EARLY):
                at = (d * 12 + f) * 24
                buffer[at : at + 24, :] = wide[first + d, f]
        first = jnp.where(east, 8 - LATE, 0)
        for d in range(LATE):
            for c in range(NC):
                at = RATIO_AT + (d * NC + c) * 16
                buffer[at : at + 8, :] = wide[first + d, 12 + c, 8:16, :]
                buffer[at + 8 : at + 16, :] = jnp.where(
                    row < 4, wide[first + d, 12 + c, 16:24, :], wide[first + d, 12 + c, 0:8, :]
                )


def north_of(tiles, row):
    south, home, north = (pltpu.roll(tile, 7, 0) for tile in tiles)
    last = row == 7
    return (jnp.where(last, home, south), jnp.where(last, north, home), north)


def south_of(tiles, row):
    south, home, north = (pltpu.roll(tile, 1, 0) for tile in tiles)
    first = row == 0
    return (south, jnp.where(first, south, home), jnp.where(first, home, north))


def early_kernel(
    wide, recv_a, recv_b, trans, gain, begin, begin_edge, iters, perms, ratios
):
    row = rows_of()
    lane = lanes_of()
    gx = lax.axis_index("gx")
    even = lax.rem(gx, 2) == 0
    west_in = (gx > 0).astype(F32)
    east_in = (gx < 7).astype(F32)

    def bring(d, _):
        for f in range(12):
            at = pl.multiple_of((d * 12 + f) * 24, 8)
            from_a = recv_a[pl.ds(at, 24), :]
            from_b = recv_b[pl.ds(at, 24), :]
            west = jnp.where(even, from_b, from_a)
            east = jnp.where(even, from_a, from_b)
            if f < NC:
                iters[d, f] = west
                iters[8 + EARLY + d, f] = east
            else:
                perms[d, f - 9] = west * west_in
                perms[8 + EARLY + d, f - 9] = east * east_in
        return 0

    lax.fori_loop(0, EARLY, bring, 0)

    def bring_ratio(d, _):
        for c in range(NC):
            at = pl.multiple_of(RATIO_AT + (d * NC + c) * 16, 8)
            from_a = recv_a[pl.ds(at, 16), :]
            from_b = recv_b[pl.ds(at, 16), :]
            ratios[d, c] = jnp.where(even, from_b, from_a)
            ratios[LATE + d, c] = jnp.where(even, from_a, from_b)
        return 0

    lax.fori_loop(0, LATE, bring_ratio, 0)

    def settle(x, _):
        for f in range(NC):
            iters[EARLY + x, f] = wide[x, f]
        for f in range(3):
            perms[EARLY + x, f] = wide[x, 9 + f]
        return 0

    lax.fori_loop(0, 8, settle, 0)

    def column(at, ratio_of):
        here = at + 1

        def three(ref, *index):
            return tuple(ref[index + (slice(8 * t, 8 * t + 8), slice(None))] for t in range(3))

        px = three(perms, here, 0)
        py = three(perms, here, 1)
        pz = three(perms, here, 2)
        t_east = [a * b for a, b in zip(px, three(perms, here + 1, 0))]
        t_west = [a * b for a, b in zip(px, three(perms, here - 1, 0))]
        t_north = [a * b for a, b in zip(py, north_of(py, row))]
        t_south = [a * b for a, b in zip(py, south_of(py, row))]
        t_up = [jnp.where(lane < 127, a * pltpu.roll(a, 127, 1), 0.0) for a in pz]
        t_down = [jnp.where(lane > 0, a * pltpu.roll(a, 1, 1), 0.0) for a in pz]
        kinds = (t_east, t_west, t_north, t_south, t_up, t_down)
        total = [sum(kind[t] for kind in kinds) for t in range(3)]

        def outer(tiles):
            return jnp.where(row < 4, tiles[2], tiles[0])

        def edge(tiles):
            return jnp.where(row == 4, tiles[2], tiles[0])

        for n, kind in enumerate(kinds):
            trans[at, n, 0:8, :] = kind[1]
            trans[at, n, 8:16, :] = outer(kind)
        for c in range(NC):
            mid = three(iters, here, c)
            east = three(iters, here + 1, c)
            west = three(iters, here - 1, c)
            north = north_of(mid, row)
            south = south_of(mid, row)
            beside = []
            for t in range(3):
                value = t_east[t] * east[t] + t_west[t] * west[t]
                value = value + t_north[t] * north[t] + t_south[t] * south[t]
                value = value + t_up[t] * pltpu.roll(mid[t], 127, 1)
                value = value + t_down[t] * pltpu.roll(mid[t], 1, 1)
                beside.append(value)
            ratio = ratio_of(c)
            scale = OMEGA / (ratio[0] + total[1])
            gain[at, c, 0:8, :] = scale
            begin[at, c, 0:8, :] = KEEP * mid[1] + scale * beside[1]
            scale = OMEGA / (ratio[1] + outer(total))
            gain[at, c, 8:16, :] = scale
            begin[at, c, 8:16, :] = KEEP * outer(mid) + scale * outer(beside)
            if ratio[2] is not None:
                scale = OMEGA / (ratio[2] + edge(total))
                begin_edge[at - LATE, c] = KEEP * edge(mid) + scale * edge(beside)

    def home_column(x, _):
        def ratio_of(c):
            south = wide[x, 12 + c, 0:8, :]
            north = wide[x, 12 + c, 16:24, :]
            return (
                wide[x, 12 + c, 8:16, :],
                jnp.where(row < 4, north, south),
                jnp.where(row == 4, north, south),
            )

        column(x + LATE, ratio_of)
        return 0

    def halo_column(d, _):
        def ratio_of(c):
            return (ratios[d, c, 0:8, :], ratios[d, c, 8:16, :], None)

        column(jnp.where(d < LATE, d, d + 8), ratio_of)
        return 0

    lax.fori_loop(0, 8, home_column, 0)
    lax.fori_loop(0, 2 * LATE, halo_column, 0)


def scatter_kernel(
    cell, arrived, wide, recv_a, recv_b, cot, accum, mobil, weight, send_a, send_b, left, right, total
):
    row = rows_of()
    lane = lanes_of()
    row16 = rows_of((16, 128))
    gx = lax.axis_index("gx")
    even_x = lax.rem(gx, 2) == 0

    def build(j, _):
        for half in range(2):
            at = pl.ds(pl.multiple_of(j * 256 + half * 128, 128), 128)
            place = cell[j, half : half + 1, :]
            place = jnp.broadcast_to(place, (16, 128))
            low = lax.bitwise_and(lax.shift_right_logical(place, 7), 15)
            high = lax.bitwise_or(
                lax.bitwise_and(place, 127),
                lax.shift_left(lax.shift_right_logical(place, 11), 7),
            )
            mine = low == row16
            values = arrived[j, pl.ds(half, NC, stride=2), :]
            coarse = values.astype(BF16).astype(F32)
            fine = values - coarse
            for c in range(NC):
                for part, source in ((0, coarse), (1, fine)):
                    line = jnp.broadcast_to(source[c : c + 1, :], (16, 128))
                    left[part * 144 + c * 16 : part * 144 + c * 16 + 16, at] = jnp.where(
                        mine, line, 0.0
                    ).astype(BF16)
            for n in range(32):
                right[n * 16 : n * 16 + 16, at] = jnp.where(
                    high == row16 + n * 16, 1.0, 0.0
                ).astype(BF16)
        return 0

    lax.fori_loop(0, BRICKS, build, 0)

    west_in = (gx > 0).astype(F32)
    east_in = (gx < 7).astype(F32)
    at_west = slice(((EARLY - 1) * 12 + 9) * 24 + 8, ((EARLY - 1) * 12 + 9) * 24 + 16)
    at_east = slice(9 * 24 + 8, 9 * 24 + 16)
    px_west = jnp.where(even_x, recv_b[at_west, :], recv_a[at_west, :]) * west_in
    px_east = jnp.where(even_x, recv_a[at_east, :], recv_b[at_east, :]) * east_in
    for x in range(8):
        px = wide[x, 9, 8:16, :]
        east = wide[x + 1, 9, 8:16, :] if x < 7 else px_east
        west = wide[x - 1, 9, 8:16, :] if x > 0 else px_west
        value = px * east + px * west
        py = tuple(wide[x, 10, 8 * t : 8 * t + 8, :] for t in range(3))
        value = value + py[1] * north_of(py, row)[1] + py[1] * south_of(py, row)[1]
        pz = wide[x, 11, 8:16, :]
        value = value + jnp.where(lane < 127, pz * pltpu.roll(pz, 127, 1), 0.0)
        value = value + jnp.where(lane > 0, pz * pltpu.roll(pz, 1, 1), 0.0)
        total[x * 8 : x * 8 + 8, :] = value

    for part in range(2):
        product = lax.dot_general(
            left[...],
            right[part * 256 : part * 256 + 256, :],
            (((1,), (1,)), ((), ())),
            preferred_element_type=F32,
        )
        for side in range(2):
            pair = part * 2 + side
            at = slice(side * 128, side * 128 + 128)
            for c in range(NC):
                well = product[c * 16 : c * 16 + 16, at] + product[144 + c * 16 : 160 + c * 16, at]
                here = slice((c * 4 + pair) * 16, (c * 4 + pair) * 16 + 16)
                diagonal = accum[here, :].astype(F32) + mobil[here, :].astype(F32) * total[
                    pair * 16 : pair * 16 + 16, :
                ]
                weight[here, :] = OMEGA * (cot[here, :].astype(F32) - well) / diagonal

    even = lax.rem(lax.axis_index("gy"), 2) == 0
    for buffer in (send_a, send_b):
        buffer[0:8, :] = jnp.zeros(TILE, F32)
        buffer[LATE_ROWS - 8 : LATE_ROWS, :] = jnp.zeros(TILE, F32)
    for i in range(NC * 8):
        low = weight[i * 8 : i * 8 + LATE, :]
        high = weight[i * 8 + 8 - LATE : i * 8 + 8, :]
        at = slice(8 + i * LATE, 8 + i * LATE + LATE)
        send_a[at, :] = jnp.where(even, high, low)
        send_b[at, :] = jnp.where(even, low, high)


def late_wide_kernel(weight, recv_a, recv_b, wide, edge, send_a, send_b):
    row = rows_of()
    even = lax.rem(lax.axis_index("gy"), 2) == 0
    for c in range(NC):
        for x in range(8):
            i = c * 8 + x
            at = 8 + i * LATE
            low = slice(at - (8 - LATE), at + LATE)
            high = slice(at, at + 8)
            south = jnp.where(even, recv_b[low, :], recv_a[low, :])
            north = jnp.where(even, recv_a[high, :], recv_b[high, :])
            wide[x, c, 0:8, :] = weight[i * 8 : i * 8 + 8, :]
            wide[x, c, 8:16, :] = jnp.where(row < 4, north, south)
            edge[x, c] = jnp.where(row == 4, north, south)
    even_x = lax.rem(lax.axis_index("gx"), 2) == 0
    for buffer, east in ((send_a, even_x), (send_b, jnp.logical_not(even_x))):
        first = jnp.where(east, 8 - LATE, 0)
        for d in range(LATE):
            for c in range(NC):
                buffer[d, c] = wide[first + d, c]


def sweep_kernel(
    trans, gain, begin, begin_edge, wide, edge, recv_a, recv_b, result, weight, one, two
):
    row = rows_of()
    even = lax.rem(lax.axis_index("gx"), 2) == 0

    def bring(d, _):
        for c in range(NC):
            from_a = recv_a[d, c]
            from_b = recv_b[d, c]
            west = jnp.where(even, from_b, from_a)
            east = jnp.where(even, from_a, from_b)
            weight[d, c] = west
            weight[8 + LATE + d, c] = east
            one[d, c] = west + begin[d, c]
            one[8 + LATE + d, c] = east + begin[8 + LATE + d, c]
        return 0

    lax.fori_loop(0, LATE, bring, 0)

    def settle(x, _):
        for c in range(NC):
            weight[LATE + x, c] = wide[x, c]
            one[LATE + x, c] = wide[x, c] + begin[LATE + x, c]
        return 0

    lax.fori_loop(0, 8, settle, 0)
    first = row == 0
    last = row == 7

    def column(at, held, new, brim, final):
        kinds = [[trans[at, n, 8 * t : 8 * t + 8, :] for t in range(2)] for n in range(6)]
        t_east, t_west, t_north, t_south, t_up, t_down = kinds
        for c in range(NC):
            mid = [held[at, c, 8 * t : 8 * t + 8, :] for t in range(2)]
            east = [held[at + 1, c, 8 * t : 8 * t + 8, :] for t in range(2)]
            west = [held[at - 1, c, 8 * t : 8 * t + 8, :] for t in range(2)]
            back = [pltpu.roll(tile, 7, 0) for tile in mid]
            fore = [pltpu.roll(tile, 1, 0) for tile in mid]
            north = [jnp.where(last, back[1], back[0]), jnp.where(last, back[0], back[1])]
            south = [jnp.where(first, fore[1], fore[0]), jnp.where(first, fore[0], fore[1])]
            if brim:
                outer = begin_edge[at - LATE, c] + edge[at - LATE, c]
                north[1] = jnp.where(row == 3, pltpu.roll(outer, 7, 0), north[1])
                south[1] = jnp.where(row == 4, pltpu.roll(outer, 1, 0), south[1])
            for t in range(1 if final else 2):
                value = t_east[t] * east[t] + t_west[t] * west[t]
                value = value + t_north[t] * north[t] + t_south[t] * south[t]
                value = value + t_up[t] * pltpu.roll(mid[t], 127, 1)
                value = value + t_down[t] * pltpu.roll(mid[t], 1, 1)
                part = slice(8 * t, 8 * t + 8)
                value = KEEP * mid[t] + weight[at, c, part, :] + gain[at, c, part, :] * value
                if final:
                    result[c, at - LATE] = value
                else:
                    new[at, c, part, :] = value

    def sweep(begin_at, end_at, held, new, brim=False, final=False):
        def body(at, _):
            column(at, held, new, brim, final)
            return 0

        lax.fori_loop(begin_at, end_at, body, 0)

    sweep(1, LATE, one, two)
    sweep(LATE, LATE + 8, one, two, brim=True)
    sweep(LATE + 8, COLS - 1, one, two)
    sweep(2, COLS - 2, two, one)
    sweep(3, COLS - 3, one, two)
    sweep(4, COLS - 4, two, one)
    sweep(5, COLS - 5, one, None, final=True)


def swap_pairs(shards, axis):
    count = lax.axis_size(axis)
    inner = [(i, i ^ 1) for i in range(count)]
    outer = [(i, (((i + 1) ^ 1) - 1) % count) for i in range(count)]
    return lax.ppermute(shards[0], axis, inner), lax.ppermute(shards[1], axis, outer)


def body(
    seg_source,
    seg_inverse,
    seg_outflow,
    well_len,
    perf_seg,
    perf_count,
    perf_coupling,
    recv_cell,
    cell_cot,
    start_iterate,
    accumulation,
    mobility,
    perm_x,
    perm_y,
    perm_z,
):
    cot = cell_cot.reshape(NC * 64, 128)
    accum = accumulation.reshape(NC * 64, 128)
    mobil = mobility.reshape(NC * 64, 128)
    ratio, early_a, early_b = call(
        early_pack_kernel,
        (out(NC * 64, 128), out(EARLY_ROWS, 128), out(EARLY_ROWS, 128)),
        [],
        [VMEM] * 6,
        "early_pack",
    )(start_iterate, perm_x, perm_y, perm_z, accum, mobil)
    early_a, early_b = swap_pairs((early_a, early_b), "gy")

    mats, vecs, head = call(
        scan_kernel,
        (out(81, 8, 128), out(NC, 8, 128), out(BRICKS, 8, 128)),
        [pltpu.VMEM((90, 8, 128), F32)],
        [SMEM, VMEM, VMEM, VMEM],
        "well_scan",
        10_000_000,
    )(well_len, seg_source, seg_inverse, seg_outflow)
    heads = lax.all_to_all(head, "gy", 0, 0, tiled=True)

    wide, wide_a, wide_b = call(
        early_wide_kernel,
        (out(8, FIELDS, 24, 128), out(WIDE_ROWS, 128), out(WIDE_ROWS, 128)),
        [],
        [VMEM] * 7,
        "early_wide",
    )(start_iterate, perm_x, perm_y, perm_z, ratio, early_a, early_b)
    wide_a, wide_b = swap_pairs((wide_a, wide_b), "gx")

    lam, sent = call(
        rows_kernel,
        (out(NC, 8, 128), out(BRICKS * SLOT, 128)),
        [],
        [SMEM] + [VMEM] * 5,
        "well_rows",
    )(
        perf_count.reshape(BRICKS),
        mats,
        vecs,
        heads,
        perf_seg.reshape(BRICKS, 256),
        perf_coupling.reshape(NC, NC, BRICKS, 256),
    )
    arrived = lax.all_to_all(sent, "gy", 0, 0, tiled=True)

    weight, late_a, late_b = call(
        scatter_kernel,
        (out(NC * 64, 128), out(LATE_ROWS, 128), out(LATE_ROWS, 128)),
        [
            pltpu.VMEM((288, 4096), BF16),
            pltpu.VMEM((512, 4096), BF16),
            pltpu.VMEM((64, 128), F32),
        ],
        [VMEM] * 8,
        "scatter",
        limit=32,
    )(recv_cell.reshape(BRICKS, 2, 128), arrived.reshape(BRICKS, SLOT, 128), wide, wide_a, wide_b, cot, accum, mobil)
    late_a, late_b = swap_pairs((late_a, late_b), "gy")

    trans, gain, begin, begin_edge = call(
        early_kernel,
        (
            out(COLS, 6, 16, 128),
            out(COLS, NC, 16, 128),
            out(COLS, NC, 16, 128),
            out(8, NC, 8, 128),
        ),
        [
            pltpu.VMEM((8 + 2 * EARLY, NC, 24, 128), F32),
            pltpu.VMEM((8 + 2 * EARLY, 3, 24, 128), F32),
            pltpu.VMEM((2 * LATE, NC, 16, 128), F32),
        ],
        [VMEM] * 3,
        "early",
        limit=24,
    )(wide, wide_a, wide_b)

    widened, edge, side_a, side_b = call(
        late_wide_kernel,
        (
            out(8, NC, 16, 128),
            out(8, NC, 8, 128),
            out(LATE, NC, 16, 128),
            out(LATE, NC, 16, 128),
        ),
        [],
        [VMEM] * 3,
        "late_wide",
    )(weight, late_a, late_b)
    side_a, side_b = swap_pairs((side_a, side_b), "gx")

    wide_field = pltpu.VMEM((COLS, NC, 16, 128), F32)
    result = call(
        sweep_kernel,
        out(NC, 8, 8, 128),
        [wide_field] * 3,
        [VMEM] * 8,
        "sweeps",
        limit=24,
    )(trans, gain, begin, begin_edge, widened, edge, side_a, side_b)
    return lam, result


def solution(mesh):
    return jax.shard_map(
        body,
        mesh=mesh,
        in_specs=(
            P(None, "gx", "gy"),
            P(None, None, "gx", "gy"),
            P(None, None, "gx", "gy"),
            P("gx"),
            P("gx", "gy", None, None),
            P("gx", "gy", None),
            P(None, None, "gx", "gy", None, None),
            P("gx", "gy", None, None),
            P(None, "gx", "gy", None),
            P(None, "gx", "gy", None),
            P(None, "gx", "gy", None),
            P(None, "gx", "gy", None),
            P("gx", "gy", None),
            P("gx", "gy", None),
            P("gx", "gy", None),
        ),
        out_specs=(P(None, "gx", "gy"), P(None, "gx", "gy", None)),
        check_vma=False,
    )
```

```python
import jax
import jax.numpy as jnp
from jax import lax
from jax.experimental import pallas as pl
from jax.experimental.pallas import tpu as pltpu
from jax.sharding import PartitionSpec as P

F32 = jnp.float32
BF16 = jnp.bfloat16
I32 = jnp.int32
NC = 9
OMEGA = 0.8
KEEP = 1.0 - OMEGA
BRICKS = 16
EARLY = 6
LATE = 5
TILE = (8, 128)
FIELDS = 21
EARLY_ROWS = 16 + FIELDS * 8 * EARLY
LATE_ROWS = 16 + NC * 8 * LATE
RATIO_AT = 12 * EARLY * 24
WIDE_ROWS = RATIO_AT + NC * LATE * 16
COLS = 8 + 2 * LATE
SLOT = 24

VMEM = pl.BlockSpec(memory_space=pltpu.VMEM)
SMEM = pl.BlockSpec(memory_space=pltpu.SMEM)
HBM = pl.BlockSpec(memory_space=pltpu.HBM)


def lanes_of(shape=TILE):
    return lax.broadcasted_iota(I32, shape, 1)


def rows_of(shape=TILE):
    return lax.broadcasted_iota(I32, shape, 0)


def call(kernel, outs, scratch, specs, name, flops=1_000_000, limit=8, out_specs=None):
    return pl.pallas_call(
        kernel,
        out_shape=outs,
        in_specs=specs,
        out_specs=jax.tree.map(lambda _: VMEM, outs) if out_specs is None else out_specs,
        scratch_shapes=scratch,
        compiler_params=pltpu.CompilerParams(vmem_limit_bytes=limit * 1024 * 1024),
        cost_estimate=pl.CostEstimate(
            flops=flops, bytes_accessed=1_000_000, transcendentals=0
        ),
        name=name,
    )


def out(*shape, dtype=F32):
    return jax.ShapeDtypeStruct(shape, dtype)


def far(*shape, dtype=F32):
    return pltpu.HBM(shape, dtype)


def pin(array):
    return pltpu.with_memory_space_constraint(array, pltpu.HBM)


def fetch(sources, targets, sems):
    copies = [
        pltpu.make_async_copy(source, target, sems.at[n])
        for n, (source, target) in enumerate(zip(sources, targets))
    ]
    for copy in copies:
        copy.start()
    return copies


def first_kernel(
    len_hbm,
    src_hbm,
    inv_hbm,
    outf_hbm,
    start_hbm,
    px_hbm,
    py_hbm,
    pz_hbm,
    accum_hbm,
    mobil_hbm,
    mats,
    vecs,
    head,
    ratio,
    send_a,
    send_b,
    edge_a,
    edge_b,
    rolled,
    len_ref,
    src,
    inv,
    outf,
    start,
    px,
    py,
    pz,
    accum,
    mobil,
    sems,
):
    copies = fetch(
        (
            inv_hbm,
            outf_hbm,
            src_hbm,
            len_hbm,
            start_hbm,
            px_hbm,
            py_hbm,
            pz_hbm,
            accum_hbm,
            mobil_hbm,
        ),
        (inv, outf, src, len_ref, start, px, py, pz, accum, mobil),
        sems,
    )
    for copy in copies[:4]:
        copy.wait()
    scan_wells(len_ref, src, inv, outf, mats, vecs, head, rolled)
    for copy in copies[4:]:
        copy.wait()
    early_pack(start, px, py, pz, accum, mobil, ratio, send_a, send_b, edge_a, edge_b)


def scan_wells(len_ref, src, inv, outf, mats, vecs, head, rolled):
    lane = lanes_of()
    well = rows_of()
    length = jnp.zeros(TILE, I32)
    for w in range(8):
        length = jnp.where(well == w, len_ref[w], length)
    active = (lax.axis_index("gy") * 128 + lane < length).astype(F32)

    def start(c, _):
        row = [inv[j, c] for j in range(NC)]
        total = row[0] * src[0]
        for j in range(1, NC):
            total = total + row[j] * src[j]
        vecs[c] = active * total
        for k in range(NC):
            total = row[0] * outf[k, 0]
            for j in range(1, NC):
                total = total + row[j] * outf[k, j]
            mats[c * NC + k] = -active * total
        return 0

    lax.fori_loop(0, NC, start, 0)

    def step(i, _):
        gap = lax.shift_left(jnp.int32(1), i)
        keep = lane < 128 - gap
        for k in range(NC):
            for m in range(NC):
                moved = pltpu.roll(mats[k * NC + m], 128 - gap, 1)
                rolled[k * 10 + m] = jnp.where(keep, moved, 1.0 if k == m else 0.0)
            rolled[k * 10 + 9] = jnp.where(keep, pltpu.roll(vecs[k], 128 - gap, 1), 0.0)

        def rows(group, _):
            rows3 = [[mats[(group * 3 + a) * NC + k] for k in range(NC)] for a in range(3)]
            for m in range(10):
                right = [rolled[k * 10 + m] for k in range(NC)]
                for a in range(3):
                    total = rows3[a][0] * right[0]
                    for k in range(1, NC):
                        total = total + rows3[a][k] * right[k]
                    if m < NC:
                        mats[(group * 3 + a) * NC + m] = total
                    else:
                        vecs[group * 3 + a] = vecs[group * 3 + a] + total
            return 0

        return lax.fori_loop(0, 3, rows, 0)

    lax.fori_loop(0, 7, step, 0)
    packed = jnp.zeros(TILE, F32)
    for e in range(81):
        moved = mats[e] if e == 0 else pltpu.roll(mats[e], e, 1)
        packed = jnp.where(lane == e, moved, packed)
    for c in range(NC):
        packed = jnp.where(lane == 81 + c, pltpu.roll(vecs[c], 81 + c, 1), packed)
    for j in range(BRICKS):
        head[j] = packed


def rows_kernel(
    count_hbm,
    seg_hbm,
    mats,
    vecs,
    heads,
    coupling,
    edge_a,
    edge_b,
    lam_hbm,
    sent_hbm,
    token,
    lam,
    sent,
    count_ref,
    perf_seg,
    sem,
    sems,
    sems_out,
):
    copies = fetch((count_hbm, seg_hbm), (count_ref, perf_seg), sems)
    row = rows_of()
    lane = lanes_of()
    me = lax.axis_index("gy")

    def hop(t, incoming):
        head = heads[BRICKS - 1 - t]
        after = []
        for c in range(NC):
            total = jnp.broadcast_to(head[:, 81 + c : 82 + c], TILE)
            for k in range(NC):
                at = c * NC + k
                total = total + jnp.broadcast_to(head[:, at : at + 1], TILE) * incoming[k]
            after.append(total)
        return tuple(after)

    nothing = tuple(jnp.zeros(TILE, F32) for _ in range(NC))
    incoming = lax.fori_loop(0, BRICKS - 1 - me, hop, nothing)
    for c in range(NC):
        total = vecs[c]
        for k in range(NC):
            total = total + mats[c * NC + k] * incoming[k]
        lam[c] = total
    moves = [pltpu.make_async_copy(lam, lam_hbm, sem)]
    moves[0].start()
    token[...] = jnp.zeros(TILE, F32)
    for copy in copies:
        copy.wait()
    for block in range(2):
        count = jnp.zeros(TILE, I32)
        for b in range(8):
            count = jnp.where(row == b, count_ref[block * 8 + b], count)
        for half in range(2):
            at = (slice(block * 8, block * 8 + 8), slice(half * 128, half * 128 + 128))
            slot = perf_seg[at]
            slot_well = lax.shift_right_logical(slot, 7)
            slot_lane = lax.bitwise_and(slot, 127)
            is_well = [slot_well == w for w in range(8)]
            picked = []
            for k in range(NC):
                total = jnp.zeros(TILE, F32)
                for w in range(8):
                    line = jnp.broadcast_to(lam[k, w : w + 1, :], TILE)
                    got = jnp.take_along_axis(line, slot_lane, axis=1)
                    total = jnp.where(is_well[w], got, total)
                picked.append(total)
            live = lane + half * 128 < count
            for c in range(NC):
                total = coupling[(0, c) + at] * picked[0]
                for k in range(1, NC):
                    total = total + coupling[(k, c) + at] * picked[k]
                total = jnp.where(live, total, 0.0)
                sent[pl.ds(block * 8 * SLOT + c * 2 + half, 8, stride=SLOT), :] = total
        part = slice(block * 8 * SLOT, block * 8 * SLOT + 8 * SLOT)
        moves.append(
            pltpu.make_async_copy(sent.at[part], sent_hbm.at[part], sems_out.at[block])
        )
        moves[-1].start()
    for move in moves:
        move.wait()


def early_pack(start, px, py, pz, accum, mobil, ratio, send_a, send_b, edge_a, edge_b):
    even_x = lax.rem(lax.axis_index("gx"), 2) == 0
    edge_a[...] = jnp.where(even_x, px[7], px[0])
    edge_b[...] = jnp.where(even_x, px[0], px[7])
    even = lax.rem(lax.axis_index("gy"), 2) == 0
    for i in range(NC * 4):
        at = slice(i * 16, i * 16 + 16)
        ratio[at, :] = accum[at, :].astype(F32) / mobil[at, :].astype(F32)
    for buffer in (send_a, send_b):
        buffer[0:8, :] = jnp.zeros(TILE, F32)
        buffer[EARLY_ROWS - 8 : EARLY_ROWS, :] = jnp.zeros(TILE, F32)
    perms = (px, py, pz)
    for f in range(FIELDS):
        for x in range(8):
            if f < NC:
                low, high = start[f, x, 0:EARLY, :], start[f, x, 8 - EARLY : 8, :]
            elif f < 12:
                low, high = perms[f - 9][x, 0:EARLY, :], perms[f - 9][x, 8 - EARLY : 8, :]
            else:
                base = ((f - 12) * 8 + x) * 8
                low, high = ratio[base : base + EARLY, :], ratio[base + 8 - EARLY : base + 8, :]
            at = 8 + (f * 8 + x) * EARLY
            send_a[at : at + EARLY, :] = jnp.where(even, high, low)
            send_b[at : at + EARLY, :] = jnp.where(even, low, high)


def shade_kernel(
    after,
    start_hbm,
    px_hbm,
    py_hbm,
    pz_hbm,
    accum_hbm,
    mobil_hbm,
    cot_hbm,
    ratio,
    recv_a,
    recv_b,
    edge_a,
    edge_b,
    wide_hbm,
    send_a_hbm,
    send_b_hbm,
    scale_hbm,
    base_hbm,
    start,
    px,
    py,
    pz,
    accum,
    mobil,
    cot,
    wide,
    send_a,
    send_b,
    scale,
    base,
    sems,
    sems_out,
):
    copies = fetch(
        (start_hbm, px_hbm, py_hbm, pz_hbm, accum_hbm, mobil_hbm, cot_hbm),
        (start, px, py, pz, accum, mobil, cot),
        sems,
    )
    for copy in copies:
        copy.wait()
    row = rows_of()
    gy = lax.axis_index("gy")
    even = lax.rem(gy, 2) == 0
    south_in = (gy > 0).astype(F32)
    north_in = (gy < BRICKS - 1).astype(F32)
    perms = (px, py, pz)
    for f in range(FIELDS):
        for x in range(8):
            at = 8 + (f * 8 + x) * EARLY
            low = slice(at - (8 - EARLY), at + EARLY)
            high = slice(at, at + 8)
            south = jnp.where(even, recv_b[low, :], recv_a[low, :])
            north = jnp.where(even, recv_a[high, :], recv_b[high, :])
            if f < NC:
                home = start[f, x]
            elif f < 12:
                home = perms[f - 9][x]
                south = south * south_in
                north = north * north_in
            else:
                start_at = ((f - 12) * 8 + x) * 8
                home = ratio[start_at : start_at + 8, :]
            wide[x, f, 0:8, :] = south
            wide[x, f, 8:16, :] = home
            wide[x, f, 16:24, :] = north
    moves = fetch((wide,), (wide_hbm,), sems_out)
    even_x = lax.rem(lax.axis_index("gx"), 2) == 0
    for buffer, east in ((send_a, even_x), (send_b, jnp.logical_not(even_x))):
        first = jnp.where(east, 8 - EARLY, 0)
        for f in range(12):
            for d in range(EARLY):
                at = (d * 12 + f) * 24
                buffer[at : at + 24, :] = wide[first + d, f]
        first = jnp.where(east, 8 - LATE, 0)
        for d in range(LATE):
            for c in range(NC):
                at = RATIO_AT + (d * NC + c) * 16
                buffer[at : at + 8, :] = wide[first + d, 12 + c, 8:16, :]
                buffer[at + 8 : at + 16, :] = jnp.where(
                    row < 4, wide[first + d, 12 + c, 16:24, :], wide[first + d, 12 + c, 0:8, :]
                )
    for n, (source, target) in enumerate(((send_a, send_a_hbm), (send_b, send_b_hbm))):
        moves.append(pltpu.make_async_copy(source, target, sems_out.at[1 + n]))
        moves[-1].start()
    gx = lax.axis_index("gx")
    px_west = jnp.where(even_x, edge_b[...], edge_a[...]) * (gx > 0).astype(F32)
    px_east = jnp.where(even_x, edge_a[...], edge_b[...]) * (gx < 7).astype(F32)
    lane = lanes_of()
    totals = []
    for x in range(8):
        east = px[x + 1] if x < 7 else px_east
        west = px[x - 1] if x > 0 else px_west
        value = px[x] * east + px[x] * west
        along = tuple(wide[x, 10, 8 * t : 8 * t + 8, :] for t in range(3))
        value = value + along[1] * north_of(along, row)[1] + along[1] * south_of(along, row)[1]
        value = value + jnp.where(lane < 127, pz[x] * pltpu.roll(pz[x], 127, 1), 0.0)
        value = value + jnp.where(lane > 0, pz[x] * pltpu.roll(pz[x], 1, 1), 0.0)
        totals.append(value)
    for pair in range(4):
        total = jnp.concatenate(totals[pair * 2 : pair * 2 + 2], axis=0)
        for c in range(NC):
            here = slice((c * 4 + pair) * 16, (c * 4 + pair) * 16 + 16)
            diagonal = accum[here, :].astype(F32) + mobil[here, :].astype(F32) * total
            inverse = OMEGA / diagonal
            scale[here, :] = inverse
            base[here, :] = inverse * cot[here, :].astype(F32)
    for n, (source, target) in enumerate(((scale, scale_hbm), (base, base_hbm))):
        moves.append(pltpu.make_async_copy(source, target, sems_out.at[3 + n]))
        moves[-1].start()
    for move in moves:
        move.wait()


def north_of(tiles, row):
    south, home, north = (pltpu.roll(tile, 7, 0) for tile in tiles)
    last = row == 7
    return (jnp.where(last, home, south), jnp.where(last, north, home), north)


def south_of(tiles, row):
    south, home, north = (pltpu.roll(tile, 1, 0) for tile in tiles)
    first = row == 0
    return (south, jnp.where(first, south, home), jnp.where(first, home, north))


def early_kernel(
    wide_hbm, recv_a, recv_b, trans, gain, begin, begin_edge, iters, perms, ratios, wide, sem
):
    copy = pltpu.make_async_copy(wide_hbm, wide, sem)
    copy.start()
    row = rows_of()
    lane = lanes_of()
    gx = lax.axis_index("gx")
    even = lax.rem(gx, 2) == 0
    west_in = (gx > 0).astype(F32)
    east_in = (gx < 7).astype(F32)

    def bring(d, _):
        for f in range(12):
            at = pl.multiple_of((d * 12 + f) * 24, 8)
            from_a = recv_a[pl.ds(at, 24), :]
            from_b = recv_b[pl.ds(at, 24), :]
            west = jnp.where(even, from_b, from_a)
            east = jnp.where(even, from_a, from_b)
            if f < NC:
                iters[d, f] = west
                iters[8 + EARLY + d, f] = east
            else:
                perms[d, f - 9] = west * west_in
                perms[8 + EARLY + d, f - 9] = east * east_in
        return 0

    lax.fori_loop(0, EARLY, bring, 0)

    def bring_ratio(d, _):
        for c in range(NC):
            at = pl.multiple_of(RATIO_AT + (d * NC + c) * 16, 8)
            from_a = recv_a[pl.ds(at, 16), :]
            from_b = recv_b[pl.ds(at, 16), :]
            ratios[d, c] = jnp.where(even, from_b, from_a)
            ratios[LATE + d, c] = jnp.where(even, from_a, from_b)
        return 0

    lax.fori_loop(0, LATE, bring_ratio, 0)
    copy.wait()

    def settle(x, _):
        for f in range(NC):
            iters[EARLY + x, f] = wide[x, f]
        for f in range(3):
            perms[EARLY + x, f] = wide[x, 9 + f]
        return 0

    lax.fori_loop(0, 8, settle, 0)

    def column(at, ratio_of):
        here = at + 1

        def three(ref, *index):
            return tuple(ref[index + (slice(8 * t, 8 * t + 8), slice(None))] for t in range(3))

        px = three(perms, here, 0)
        py = three(perms, here, 1)
        pz = three(perms, here, 2)
        t_east = [a * b for a, b in zip(px, three(perms, here + 1, 0))]
        t_west = [a * b for a, b in zip(px, three(perms, here - 1, 0))]
        t_north = [a * b for a, b in zip(py, north_of(py, row))]
        t_south = [a * b for a, b in zip(py, south_of(py, row))]
        t_up = [jnp.where(lane < 127, a * pltpu.roll(a, 127, 1), 0.0) for a in pz]
        t_down = [jnp.where(lane > 0, a * pltpu.roll(a, 1, 1), 0.0) for a in pz]
        kinds = (t_east, t_west, t_north, t_south, t_up, t_down)
        total = [sum(kind[t] for kind in kinds) for t in range(3)]

        def outer(tiles):
            return jnp.where(row < 4, tiles[2], tiles[0])

        def edge(tiles):
            return jnp.where(row == 4, tiles[2], tiles[0])

        for n, kind in enumerate(kinds):
            trans[at, n, 0:8, :] = kind[1]
            trans[at, n, 8:16, :] = outer(kind)
        for c in range(NC):
            mid = three(iters, here, c)
            east = three(iters, here + 1, c)
            west = three(iters, here - 1, c)
            north = north_of(mid, row)
            south = south_of(mid, row)
            beside = []
            for t in range(3):
                value = t_east[t] * east[t] + t_west[t] * west[t]
                value = value + t_north[t] * north[t] + t_south[t] * south[t]
                value = value + t_up[t] * pltpu.roll(mid[t], 127, 1)
                value = value + t_down[t] * pltpu.roll(mid[t], 1, 1)
                beside.append(value)
            ratio = ratio_of(c)
            scale = OMEGA / (ratio[0] + total[1])
            gain[at, c, 0:8, :] = scale
            begin[at, c, 0:8, :] = KEEP * mid[1] + scale * beside[1]
            scale = OMEGA / (ratio[1] + outer(total))
            gain[at, c, 8:16, :] = scale
            begin[at, c, 8:16, :] = KEEP * outer(mid) + scale * outer(beside)
            if ratio[2] is not None:
                scale = OMEGA / (ratio[2] + edge(total))
                begin_edge[at - LATE, c] = KEEP * edge(mid) + scale * edge(beside)

    def home_column(x, _):
        def ratio_of(c):
            south = wide[x, 12 + c, 0:8, :]
            north = wide[x, 12 + c, 16:24, :]
            return (
                wide[x, 12 + c, 8:16, :],
                jnp.where(row < 4, north, south),
                jnp.where(row == 4, north, south),
            )

        column(x + LATE, ratio_of)
        return 0

    def halo_column(d, _):
        def ratio_of(c):
            return (ratios[d, c, 0:8, :], ratios[d, c, 8:16, :], None)

        column(jnp.where(d < LATE, d, d + 8), ratio_of)
        return 0

    lax.fori_loop(0, 8, home_column, 0)
    lax.fori_loop(0, 2 * LATE, halo_column, 0)


def scatter_kernel(
    cell,
    arrived,
    scale_hbm,
    base_hbm,
    weight,
    send_a,
    send_b,
    left,
    right,
    scale,
    base,
    sems,
):
    copies = fetch(
        (scale_hbm, base_hbm),
        (scale, base),
        sems,
    )
    row16 = rows_of((16, 128))

    def mark(j, _):
        for half in range(2):
            at = pl.ds(pl.multiple_of(j * 256 + half * 128, 128), 128)
            place = jnp.broadcast_to(cell[j, half : half + 1, :], (16, 128))
            high = lax.bitwise_or(
                lax.bitwise_and(place, 127),
                lax.shift_left(lax.shift_right_logical(place, 11), 7),
            )
            for n in range(32):
                right[n * 16 : n * 16 + 16, at] = jnp.where(
                    high == row16 + n * 16, 1.0, 0.0
                ).astype(BF16)
        return 0

    lax.fori_loop(0, BRICKS, mark, 0)
    def build(j, _):
        for half in range(2):
            at = pl.ds(pl.multiple_of(j * 256 + half * 128, 128), 128)
            place = cell[j, half : half + 1, :]
            place = jnp.broadcast_to(place, (16, 128))
            low = lax.bitwise_and(lax.shift_right_logical(place, 7), 15)
            mine = low == row16
            values = arrived[j, pl.ds(half, NC, stride=2), :]
            coarse = values.astype(BF16).astype(F32)
            fine = values - coarse
            for c in range(NC):
                for part, source in ((0, coarse), (1, fine)):
                    line = jnp.broadcast_to(source[c : c + 1, :], (16, 128))
                    left[part * 144 + c * 16 : part * 144 + c * 16 + 16, at] = jnp.where(
                        mine, line, 0.0
                    ).astype(BF16)
        return 0

    lax.fori_loop(0, BRICKS, build, 0)

    for part in range(2):
        if part == 0:
            copies[0].wait()
            copies[1].wait()
        product = lax.dot_general(
            left[...],
            right[part * 256 : part * 256 + 256, :],
            (((1,), (1,)), ((), ())),
            preferred_element_type=F32,
        )
        for side in range(2):
            pair = part * 2 + side
            at = slice(side * 128, side * 128 + 128)
            for c in range(NC):
                well = product[c * 16 : c * 16 + 16, at] + product[144 + c * 16 : 160 + c * 16, at]
                here = slice((c * 4 + pair) * 16, (c * 4 + pair) * 16 + 16)
                weight[here, :] = base[here, :] - scale[here, :] * well

    even = lax.rem(lax.axis_index("gy"), 2) == 0
    for buffer in (send_a, send_b):
        buffer[0:8, :] = jnp.zeros(TILE, F32)
        buffer[LATE_ROWS - 8 : LATE_ROWS, :] = jnp.zeros(TILE, F32)
    for i in range(NC * 8):
        low = weight[i * 8 : i * 8 + LATE, :]
        high = weight[i * 8 + 8 - LATE : i * 8 + 8, :]
        at = slice(8 + i * LATE, 8 + i * LATE + LATE)
        send_a[at, :] = jnp.where(even, high, low)
        send_b[at, :] = jnp.where(even, low, high)


def late_wide_kernel(weight, recv_a, recv_b, wide, edge, send_a, send_b):
    row = rows_of()
    even = lax.rem(lax.axis_index("gy"), 2) == 0
    for c in range(NC):
        for x in range(8):
            i = c * 8 + x
            at = 8 + i * LATE
            low = slice(at - (8 - LATE), at + LATE)
            high = slice(at, at + 8)
            south = jnp.where(even, recv_b[low, :], recv_a[low, :])
            north = jnp.where(even, recv_a[high, :], recv_b[high, :])
            wide[x, c, 0:8, :] = weight[i * 8 : i * 8 + 8, :]
            wide[x, c, 8:16, :] = jnp.where(row < 4, north, south)
            edge[x, c] = jnp.where(row == 4, north, south)
    even_x = lax.rem(lax.axis_index("gx"), 2) == 0
    for buffer, east in ((send_a, even_x), (send_b, jnp.logical_not(even_x))):
        first = jnp.where(east, 8 - LATE, 0)
        for d in range(LATE):
            for c in range(NC):
                buffer[d, c] = wide[first + d, c]


def sweep_kernel(
    trans, gain, begin, begin_edge, wide, edge, recv_a, recv_b, result, weight, one, two, last_one, sems
):
    row = rows_of()
    even = lax.rem(lax.axis_index("gx"), 2) == 0

    def bring(d, _):
        for c in range(NC):
            from_a = recv_a[d, c]
            from_b = recv_b[d, c]
            west = jnp.where(even, from_b, from_a)
            east = jnp.where(even, from_a, from_b)
            weight[d, c] = west
            weight[8 + LATE + d, c] = east
            one[d, c] = west + begin[d, c]
            one[8 + LATE + d, c] = east + begin[8 + LATE + d, c]
        return 0

    lax.fori_loop(0, LATE, bring, 0)

    def settle(x, _):
        for c in range(NC):
            weight[LATE + x, c] = wide[x, c]
            one[LATE + x, c] = wide[x, c] + begin[LATE + x, c]
        return 0

    lax.fori_loop(0, 8, settle, 0)
    first = row == 0
    last = row == 7

    def column(at, held, new, brim, final):
        kinds = [[trans[at, n, 8 * t : 8 * t + 8, :] for t in range(2)] for n in range(6)]
        t_east, t_west, t_north, t_south, t_up, t_down = kinds
        for c in range(NC):
            mid = [held[at, c, 8 * t : 8 * t + 8, :] for t in range(2)]
            east = [held[at + 1, c, 8 * t : 8 * t + 8, :] for t in range(2)]
            west = [held[at - 1, c, 8 * t : 8 * t + 8, :] for t in range(2)]
            back = [pltpu.roll(tile, 7, 0) for tile in mid]
            fore = [pltpu.roll(tile, 1, 0) for tile in mid]
            north = [jnp.where(last, back[1], back[0]), jnp.where(last, back[0], back[1])]
            south = [jnp.where(first, fore[1], fore[0]), jnp.where(first, fore[0], fore[1])]
            if brim:
                outer = begin_edge[at - LATE, c] + edge[at - LATE, c]
                north[1] = jnp.where(row == 3, pltpu.roll(outer, 7, 0), north[1])
                south[1] = jnp.where(row == 4, pltpu.roll(outer, 1, 0), south[1])
            for t in range(1 if final else 2):
                value = t_east[t] * east[t] + t_west[t] * west[t]
                value = value + t_north[t] * north[t] + t_south[t] * south[t]
                value = value + t_up[t] * pltpu.roll(mid[t], 127, 1)
                value = value + t_down[t] * pltpu.roll(mid[t], 1, 1)
                part = slice(8 * t, 8 * t + 8)
                value = KEEP * mid[t] + weight[at, c, part, :] + gain[at, c, part, :] * value
                if final:
                    last_one[at - LATE, c] = value
                else:
                    new[at, c, part, :] = value

    def writing(x):
        return pltpu.make_async_copy(last_one.at[x], result.at[:, x], sems.at[x])

    def sweep(begin_at, end_at, held, new, brim=False, final=False):
        def body(at, _):
            column(at, held, new, brim, final)
            if final:
                writing(at - LATE).start()
            return 0

        lax.fori_loop(begin_at, end_at, body, 0)

    sweep(1, LATE, one, two)
    sweep(LATE, LATE + 8, one, two, brim=True)
    sweep(LATE + 8, COLS - 1, one, two)
    sweep(2, COLS - 2, two, one)
    sweep(3, COLS - 3, one, two)
    sweep(4, COLS - 4, two, one)
    sweep(5, COLS - 5, one, None, final=True)
    for x in range(8):
        writing(x).wait()


def swap_pairs(shards, axis):
    count = lax.axis_size(axis)
    inner = [(i, i ^ 1) for i in range(count)]
    outer = [(i, (((i + 1) ^ 1) - 1) % count) for i in range(count)]
    return lax.ppermute(shards[0], axis, inner), lax.ppermute(shards[1], axis, outer)


def body(
    seg_source,
    seg_inverse,
    seg_outflow,
    well_len,
    perf_seg,
    perf_count,
    perf_coupling,
    recv_cell,
    cell_cot,
    start_iterate,
    accumulation,
    mobility,
    perm_x,
    perm_y,
    perm_z,
):
    cot = cell_cot.reshape(NC * 64, 128)
    accum = accumulation.reshape(NC * 64, 128)
    mobil = mobility.reshape(NC * 64, 128)
    held = [
        pltpu.VMEM((NC, 8, 8, 128), F32),
        pltpu.VMEM((8, 8, 128), F32),
        pltpu.VMEM((8, 8, 128), F32),
        pltpu.VMEM((8, 8, 128), F32),
        pltpu.VMEM((NC * 64, 128), BF16),
        pltpu.VMEM((NC * 64, 128), BF16),
    ]
    given = [pin(x) for x in (start_iterate, perm_x, perm_y, perm_z, accum, mobil)]
    mats, vecs, head, ratio, early_a, early_b, edge_a, edge_b = call(
        first_kernel,
        (
            out(81, 8, 128),
            out(NC, 8, 128),
            out(BRICKS, 8, 128),
            out(NC * 64, 128),
            out(EARLY_ROWS, 128),
            out(EARLY_ROWS, 128),
            out(8, 128),
            out(8, 128),
        ),
        [
            pltpu.VMEM((90, 8, 128), F32),
            pltpu.SMEM((8,), I32),
            pltpu.VMEM((NC, 8, 128), F32),
            pltpu.VMEM((NC, NC, 8, 128), F32),
            pltpu.VMEM((NC, NC, 8, 128), F32),
        ]
        + held
        + [pltpu.SemaphoreType.DMA((10,))],
        [HBM] * 10,
        "first",
        10_000_000,
    )(pin(well_len), pin(seg_source), pin(seg_inverse), pin(seg_outflow), *given)
    heads = lax.all_to_all(head, "gy", 0, 0, tiled=True)
    early_a, early_b = swap_pairs((early_a, early_b), "gy")
    edge_a, edge_b = swap_pairs((edge_a, edge_b), "gx")

    lam, sent, token = call(
        rows_kernel,
        (far(NC, 8, 128), far(BRICKS * SLOT, 128), out(8, 128)),
        [
            pltpu.VMEM((NC, 8, 128), F32),
            pltpu.VMEM((BRICKS * SLOT, 128), F32),
            pltpu.SMEM((BRICKS,), I32),
            pltpu.VMEM((BRICKS, 256), I32),
            pltpu.SemaphoreType.DMA,
            pltpu.SemaphoreType.DMA((2,)),
            pltpu.SemaphoreType.DMA((2,)),
        ],
        [HBM, HBM] + [VMEM] * 6,
        "well_rows",
        out_specs=(HBM, HBM, VMEM),
    )(
        pin(perf_count.reshape(BRICKS)),
        pin(perf_seg.reshape(BRICKS, 256)),
        mats,
        vecs,
        heads,
        perf_coupling.reshape(NC, NC, BRICKS, 256),
        edge_a,
        edge_b,
    )
    arrived = lax.all_to_all(sent, "gy", 0, 0, tiled=True)

    cell = recv_cell.reshape(BRICKS, 2, 128)
    wide, wide_a, wide_b, scale, base = call(
        shade_kernel,
        (
            far(8, FIELDS, 24, 128),
            far(WIDE_ROWS, 128),
            far(WIDE_ROWS, 128),
            far(NC * 64, 128),
            far(NC * 64, 128),
        ),
        held
        + [
            pltpu.VMEM((NC * 64, 128), BF16),
            pltpu.VMEM((8, FIELDS, 24, 128), F32),
            pltpu.VMEM((WIDE_ROWS, 128), F32),
            pltpu.VMEM((WIDE_ROWS, 128), F32),
            pltpu.VMEM((NC * 64, 128), F32),
            pltpu.VMEM((NC * 64, 128), F32),
            pltpu.SemaphoreType.DMA((7,)),
            pltpu.SemaphoreType.DMA((5,)),
        ],
        [VMEM] + [HBM] * 7 + [VMEM] * 5,
        "shade",
        limit=12,
        out_specs=(HBM,) * 5,
    )(token, *given, pin(cot), ratio, early_a, early_b, edge_a, edge_b)
    wide_a, wide_b = swap_pairs((wide_a, wide_b), "gx")

    weight, late_a, late_b = call(
        scatter_kernel,
        (out(NC * 64, 128), out(LATE_ROWS, 128), out(LATE_ROWS, 128)),
        [
            pltpu.VMEM((288, 4096), BF16),
            pltpu.VMEM((512, 4096), BF16),
            pltpu.VMEM((NC * 64, 128), F32),
            pltpu.VMEM((NC * 64, 128), F32),
            pltpu.SemaphoreType.DMA((2,)),
        ],
        [VMEM] * 2 + [HBM] * 2,
        "scatter",
        20_000_000_000,
        limit=16,
    )(cell, arrived.reshape(BRICKS, SLOT, 128), pin(scale), pin(base))
    late_a, late_b = swap_pairs((late_a, late_b), "gy")

    trans, gain, begin, begin_edge = call(
        early_kernel,
        (
            out(COLS, 6, 16, 128),
            out(COLS, NC, 16, 128),
            out(COLS, NC, 16, 128),
            out(8, NC, 8, 128),
        ),
        [
            pltpu.VMEM((8 + 2 * EARLY, NC, 24, 128), F32),
            pltpu.VMEM((8 + 2 * EARLY, 3, 24, 128), F32),
            pltpu.VMEM((2 * LATE, NC, 16, 128), F32),
            pltpu.VMEM((8, FIELDS, 24, 128), F32),
            pltpu.SemaphoreType.DMA,
        ],
        [HBM, VMEM, VMEM],
        "early",
        limit=10,
    )(pin(wide), wide_a, wide_b)

    widened, edge, side_a, side_b = call(
        late_wide_kernel,
        (
            out(8, NC, 16, 128),
            out(8, NC, 8, 128),
            out(LATE, NC, 16, 128),
            out(LATE, NC, 16, 128),
        ),
        [],
        [VMEM] * 3,
        "late_wide",
    )(weight, late_a, late_b)
    side_a, side_b = swap_pairs((side_a, side_b), "gx")

    wide_field = pltpu.VMEM((COLS, NC, 16, 128), F32)
    result = call(
        sweep_kernel,
        out(NC, 8, 8, 128),
        [wide_field] * 3
        + [pltpu.VMEM((8, NC, 8, 128), F32), pltpu.SemaphoreType.DMA((8,))],
        [VMEM] * 8,
        "sweeps",
        out_specs=HBM,
    )(trans, gain, begin, begin_edge, widened, edge, side_a, side_b)
    return lam, result


def solution(mesh):
    return jax.shard_map(
        body,
        mesh=mesh,
        in_specs=(
            P(None, "gx", "gy"),
            P(None, None, "gx", "gy"),
            P(None, None, "gx", "gy"),
            P("gx"),
            P("gx", "gy", None, None),
            P("gx", "gy", None),
            P(None, None, "gx", "gy", None, None),
            P("gx", "gy", None, None),
            P(None, "gx", "gy", None),
            P(None, "gx", "gy", None),
            P(None, "gx", "gy", None),
            P(None, "gx", "gy", None),
            P("gx", "gy", None),
            P("gx", "gy", None),
            P("gx", "gy", None),
        ),
        out_specs=(P(None, "gx", "gy"), P(None, "gx", "gy", None)),
        check_vma=False,
    )
```

```python
import jax
import jax.numpy as jnp
from jax import lax
from jax.experimental import pallas as pl
from jax.experimental.pallas import tpu as pltpu
from jax.sharding import PartitionSpec as P

F32 = jnp.float32
BF16 = jnp.bfloat16
I32 = jnp.int32
NC = 9
OMEGA = 0.8
KEEP = 1.0 - OMEGA
BRICKS = 16
EARLY = 6
LATE = 5
TILE = (8, 128)
FIELDS = 21
EARLY_ROWS = 16 + FIELDS * 8 * EARLY
LATE_ROWS = 16 + NC * 8 * LATE
SIDE_RATIO = 12 * EARLY * 8
SIDE_ROWS = SIDE_RATIO + NC * LATE * 8
CORNER_RATIO = 12 * EARLY * 16
CORNER_ROWS = CORNER_RATIO + NC * LATE * 8
COLS = 8 + 2 * LATE
SLOT = 24

VMEM = pl.BlockSpec(memory_space=pltpu.VMEM)
SMEM = pl.BlockSpec(memory_space=pltpu.SMEM)
HBM = pl.BlockSpec(memory_space=pltpu.HBM)


def lanes_of(shape=TILE):
    return lax.broadcasted_iota(I32, shape, 1)


def rows_of(shape=TILE):
    return lax.broadcasted_iota(I32, shape, 0)


def call(kernel, outs, scratch, specs, name, flops=1_000_000, limit=8, out_specs=None):
    return pl.pallas_call(
        kernel,
        out_shape=outs,
        in_specs=specs,
        out_specs=jax.tree.map(lambda _: VMEM, outs) if out_specs is None else out_specs,
        scratch_shapes=scratch,
        compiler_params=pltpu.CompilerParams(vmem_limit_bytes=limit * 1024 * 1024),
        cost_estimate=pl.CostEstimate(
            flops=flops, bytes_accessed=1_000_000, transcendentals=0
        ),
        name=name,
    )


def out(*shape, dtype=F32):
    return jax.ShapeDtypeStruct(shape, dtype)


def far(*shape, dtype=F32):
    return pltpu.HBM(shape, dtype)


def pin(array):
    return pltpu.with_memory_space_constraint(array, pltpu.HBM)


def fetch(sources, targets, sems):
    copies = [
        pltpu.make_async_copy(source, target, sems.at[n])
        for n, (source, target) in enumerate(zip(sources, targets))
    ]
    for copy in copies:
        copy.start()
    return copies


def first_kernel(
    len_hbm,
    src_hbm,
    inv_hbm,
    outf_hbm,
    start_hbm,
    px_hbm,
    py_hbm,
    pz_hbm,
    accum_hbm,
    mobil_hbm,
    mats,
    vecs,
    head_hbm,
    ratio,
    send_a_hbm,
    send_b_hbm,
    side_a_hbm,
    side_b_hbm,
    rolled,
    head,
    send_a,
    send_b,
    side_a,
    side_b,
    len_ref,
    src,
    inv,
    outf,
    start,
    px,
    py,
    pz,
    accum,
    mobil,
    sems,
    sems_out,
):
    copies = fetch(
        (
            inv_hbm,
            outf_hbm,
            src_hbm,
            len_hbm,
            start_hbm,
            px_hbm,
            py_hbm,
            pz_hbm,
            accum_hbm,
            mobil_hbm,
        ),
        (inv, outf, src, len_ref, start, px, py, pz, accum, mobil),
        sems,
    )
    for copy in copies[4:]:
        copy.wait()
    early_pack(start, px, py, pz, accum, mobil, ratio, send_a, send_b, side_a, side_b)
    moves = fetch(
        (send_a, send_b, side_a, side_b),
        (send_a_hbm, send_b_hbm, side_a_hbm, side_b_hbm),
        sems_out,
    )
    for copy in copies[:4]:
        copy.wait()
    scan_wells(len_ref, src, inv, outf, mats, vecs, head, rolled)
    moves.append(pltpu.make_async_copy(head, head_hbm, sems_out.at[4]))
    moves[-1].start()
    for move in moves:
        move.wait()


def scan_wells(len_ref, src, inv, outf, mats, vecs, head, rolled):
    lane = lanes_of()
    well = rows_of()
    length = jnp.zeros(TILE, I32)
    for w in range(8):
        length = jnp.where(well == w, len_ref[w], length)
    active = (lax.axis_index("gy") * 128 + lane < length).astype(F32)

    def start(c, _):
        row = [inv[j, c] for j in range(NC)]
        total = row[0] * src[0]
        for j in range(1, NC):
            total = total + row[j] * src[j]
        vecs[c] = active * total
        for k in range(NC):
            total = row[0] * outf[k, 0]
            for j in range(1, NC):
                total = total + row[j] * outf[k, j]
            mats[c * NC + k] = -active * total
        return 0

    def starts(group, _):
        for a in range(3):
            start(group * 3 + a, 0)
        return 0

    lax.fori_loop(0, 3, starts, 0)

    def step(i, _):
        gap = lax.shift_left(jnp.int32(1), i)
        keep = lane < 128 - gap
        for k in range(NC):
            for m in range(NC):
                moved = pltpu.roll(mats[k * NC + m], 128 - gap, 1)
                rolled[k * 10 + m] = jnp.where(keep, moved, 1.0 if k == m else 0.0)
            rolled[k * 10 + 9] = jnp.where(keep, pltpu.roll(vecs[k], 128 - gap, 1), 0.0)

        def rows(group, _):
            rows3 = [[mats[(group * 3 + a) * NC + k] for k in range(NC)] for a in range(3)]
            for m in range(10):
                right = [rolled[k * 10 + m] for k in range(NC)]
                for a in range(3):
                    total = rows3[a][0] * right[0]
                    for k in range(1, NC):
                        total = total + rows3[a][k] * right[k]
                    if m < NC:
                        mats[(group * 3 + a) * NC + m] = total
                    else:
                        vecs[group * 3 + a] = vecs[group * 3 + a] + total
            return 0

        for group in range(3):
            rows(group, 0)
        return 0

    lax.fori_loop(0, 7, step, 0)
    packed = jnp.zeros(TILE, F32)
    for e in range(81):
        moved = mats[e] if e == 0 else pltpu.roll(mats[e], e, 1)
        packed = jnp.where(lane == e, moved, packed)
    for c in range(NC):
        packed = jnp.where(lane == 81 + c, pltpu.roll(vecs[c], 81 + c, 1), packed)
    for j in range(BRICKS):
        head[j] = packed


def rows_kernel(
    count_hbm,
    seg_hbm,
    coupling_hbm,
    mats,
    vecs,
    heads,
    lam_hbm,
    sent_hbm,
    token,
    lam,
    sent,
    count_ref,
    perf_seg,
    coupling,
    sem,
    sems,
    sems_out,
):
    copies = fetch(
        (count_hbm, seg_hbm, coupling_hbm), (count_ref, perf_seg, coupling), sems
    )
    row = rows_of()
    lane = lanes_of()
    me = lax.axis_index("gy")

    def hop(j, incoming):
        head = heads[j]
        later = j > me
        after = []
        for c in range(NC):
            total = jnp.broadcast_to(head[:, 81 + c : 82 + c], TILE)
            for k in range(NC):
                at = c * NC + k
                total = total + jnp.broadcast_to(head[:, at : at + 1], TILE) * incoming[k]
            after.append(total)
        return tuple(jnp.where(later, new, old) for new, old in zip(after, incoming))

    def hops(t, incoming):
        for step in range(5):
            incoming = hop(BRICKS - 1 - t * 5 - step, incoming)
        return incoming

    incoming = tuple(jnp.zeros(TILE, F32) for _ in range(NC))
    incoming = lax.fori_loop(0, 3, hops, incoming)
    for c in range(NC):
        total = vecs[c]
        for k in range(NC):
            total = total + mats[c * NC + k] * incoming[k]
        lam[c] = total
    moves = [pltpu.make_async_copy(lam, lam_hbm, sem)]
    moves[0].start()
    token[...] = jnp.zeros(TILE, F32)
    copies[0].wait()
    copies[1].wait()
    for block in range(2):
        count = jnp.zeros(TILE, I32)
        for b in range(8):
            count = jnp.where(row == b, count_ref[block * 8 + b], count)
        for half in range(2):
            at = (slice(block * 8, block * 8 + 8), slice(half * 128, half * 128 + 128))
            slot = perf_seg[at]
            slot_well = lax.shift_right_logical(slot, 7)
            slot_lane = lax.bitwise_and(slot, 127)
            is_well = [slot_well == w for w in range(8)]
            picked = []
            for k in range(NC):
                total = jnp.zeros(TILE, F32)
                for w in range(8):
                    line = jnp.broadcast_to(lam[k, w : w + 1, :], TILE)
                    got = jnp.take_along_axis(line, slot_lane, axis=1)
                    total = jnp.where(is_well[w], got, total)
                picked.append(total)
            live = lane + half * 128 < count
            if block == 0 and half == 0:
                copies[2].wait()
            for c in range(NC):
                total = coupling[(0, c) + at] * picked[0]
                for k in range(1, NC):
                    total = total + coupling[(k, c) + at] * picked[k]
                total = jnp.where(live, total, 0.0)
                sent[pl.ds(block * 8 * SLOT + c * 2 + half, 8, stride=SLOT), :] = total
        part = slice(block * 8 * SLOT, block * 8 * SLOT + 8 * SLOT)
        moves.append(
            pltpu.make_async_copy(sent.at[part], sent_hbm.at[part], sems_out.at[block])
        )
        moves[-1].start()
    for move in moves:
        move.wait()


def early_pack(start, px, py, pz, accum, mobil, ratio, send_a, send_b, side_a, side_b):
    even = lax.rem(lax.axis_index("gy"), 2) == 0
    for i in range(NC * 4):
        at = slice(i * 16, i * 16 + 16)
        ratio[at, :] = accum[at, :].astype(F32) / mobil[at, :].astype(F32)
    for buffer in (send_a, send_b):
        buffer[0:8, :] = jnp.zeros(TILE, F32)
        buffer[EARLY_ROWS - 8 : EARLY_ROWS, :] = jnp.zeros(TILE, F32)
    perms = (px, py, pz)
    for f in range(FIELDS):
        for x in range(8):
            if f < NC:
                low, high = start[f, x, 0:EARLY, :], start[f, x, 8 - EARLY : 8, :]
            elif f < 12:
                low, high = perms[f - 9][x, 0:EARLY, :], perms[f - 9][x, 8 - EARLY : 8, :]
            else:
                base = ((f - 12) * 8 + x) * 8
                low, high = ratio[base : base + EARLY, :], ratio[base + 8 - EARLY : base + 8, :]
            at = 8 + (f * 8 + x) * EARLY
            send_a[at : at + EARLY, :] = jnp.where(even, high, low)
            send_b[at : at + EARLY, :] = jnp.where(even, low, high)
    even_x = lax.rem(lax.axis_index("gx"), 2) == 0
    for buffer, east in ((side_a, even_x), (side_b, jnp.logical_not(even_x))):
        first = jnp.where(east, 8 - EARLY, 0)
        for d in range(EARLY):
            for f in range(12):
                at = (d * 12 + f) * 8
                tile = start[f, first + d] if f < NC else perms[f - 9][first + d]
                buffer[at : at + 8, :] = tile
        first = jnp.where(east, 8 - LATE, 0)
        for d in range(LATE):
            for c in range(NC):
                at = SIDE_RATIO + (d * NC + c) * 8
                base = pl.multiple_of((c * 8 + d + first) * 8, 8)
                buffer[at : at + 8, :] = ratio[pl.ds(base, 8), :]


def shade_kernel(
    after,
    start_hbm,
    px_hbm,
    py_hbm,
    pz_hbm,
    accum_hbm,
    mobil_hbm,
    cot_hbm,
    ratio,
    recv_a,
    recv_b,
    side_a,
    side_b,
    wide_hbm,
    send_a_hbm,
    send_b_hbm,
    scale_hbm,
    base_hbm,
    start,
    px,
    py,
    pz,
    accum,
    mobil,
    cot,
    wide,
    send_a,
    send_b,
    scale,
    base,
    sems,
    sems_out,
):
    copies = fetch(
        (start_hbm, px_hbm, py_hbm, pz_hbm, accum_hbm, mobil_hbm, cot_hbm),
        (start, px, py, pz, accum, mobil, cot),
        sems,
    )
    for copy in copies:
        copy.wait()
    row = rows_of()
    gy = lax.axis_index("gy")
    even = lax.rem(gy, 2) == 0
    south_in = (gy > 0).astype(F32)
    north_in = (gy < BRICKS - 1).astype(F32)
    perms = (px, py, pz)
    for f in range(FIELDS):
        for x in range(8):
            at = 8 + (f * 8 + x) * EARLY
            low = slice(at - (8 - EARLY), at + EARLY)
            high = slice(at, at + 8)
            south = jnp.where(even, recv_b[low, :], recv_a[low, :])
            north = jnp.where(even, recv_a[high, :], recv_b[high, :])
            if f < NC:
                home = start[f, x]
            elif f < 12:
                home = perms[f - 9][x]
                south = south * south_in
                north = north * north_in
            else:
                start_at = ((f - 12) * 8 + x) * 8
                home = ratio[start_at : start_at + 8, :]
            wide[x, f, 0:8, :] = south
            wide[x, f, 8:16, :] = home
            wide[x, f, 16:24, :] = north
    moves = fetch((wide,), (wide_hbm,), sems_out)
    even_x = lax.rem(lax.axis_index("gx"), 2) == 0
    for buffer, east in ((send_a, even_x), (send_b, jnp.logical_not(even_x))):
        first = jnp.where(east, 8 - EARLY, 0)
        for f in range(12):
            for d in range(EARLY):
                at = (d * 12 + f) * 16
                buffer[at : at + 8, :] = wide[first + d, f, 0:8, :]
                buffer[at + 8 : at + 16, :] = wide[first + d, f, 16:24, :]
        first = jnp.where(east, 8 - LATE, 0)
        for d in range(LATE):
            for c in range(NC):
                at = CORNER_RATIO + (d * NC + c) * 8
                buffer[at : at + 8, :] = jnp.where(
                    row < 4, wide[first + d, 12 + c, 16:24, :], wide[first + d, 12 + c, 0:8, :]
                )
    for n, (source, target) in enumerate(((send_a, send_a_hbm), (send_b, send_b_hbm))):
        moves.append(pltpu.make_async_copy(source, target, sems_out.at[1 + n]))
        moves[-1].start()
    gx = lax.axis_index("gx")
    west_at = slice(((EARLY - 1) * 12 + 9) * 8, ((EARLY - 1) * 12 + 10) * 8)
    east_at = slice(9 * 8, 10 * 8)
    px_west = jnp.where(even_x, side_b[west_at, :], side_a[west_at, :])
    px_west = px_west * (gx > 0).astype(F32)
    px_east = jnp.where(even_x, side_a[east_at, :], side_b[east_at, :])
    px_east = px_east * (gx < 7).astype(F32)
    lane = lanes_of()
    totals = []
    for x in range(8):
        east = px[x + 1] if x < 7 else px_east
        west = px[x - 1] if x > 0 else px_west
        value = px[x] * east + px[x] * west
        along = tuple(wide[x, 10, 8 * t : 8 * t + 8, :] for t in range(3))
        value = value + along[1] * north_of(along, row)[1] + along[1] * south_of(along, row)[1]
        value = value + jnp.where(lane < 127, pz[x] * pltpu.roll(pz[x], 127, 1), 0.0)
        value = value + jnp.where(lane > 0, pz[x] * pltpu.roll(pz[x], 1, 1), 0.0)
        totals.append(value)
    for pair in range(4):
        total = jnp.concatenate(totals[pair * 2 : pair * 2 + 2], axis=0)
        for c in range(NC):
            here = slice((c * 4 + pair) * 16, (c * 4 + pair) * 16 + 16)
            diagonal = accum[here, :].astype(F32) + mobil[here, :].astype(F32) * total
            inverse = OMEGA / diagonal
            scale[here, :] = inverse
            base[here, :] = inverse * cot[here, :].astype(F32)
    for n, (source, target) in enumerate(((scale, scale_hbm), (base, base_hbm))):
        moves.append(pltpu.make_async_copy(source, target, sems_out.at[3 + n]))
        moves[-1].start()
    for move in moves:
        move.wait()


def north_of(tiles, row):
    south, home, north = (pltpu.roll(tile, 7, 0) for tile in tiles)
    last = row == 7
    return (jnp.where(last, home, south), jnp.where(last, north, home), north)


def south_of(tiles, row):
    south, home, north = (pltpu.roll(tile, 1, 0) for tile in tiles)
    first = row == 0
    return (south, jnp.where(first, south, home), jnp.where(first, home, north))


def early_kernel(
    wide_hbm,
    side_a,
    side_b,
    corner_a,
    corner_b,
    trans,
    gain,
    begin,
    begin_edge,
    iters,
    perms,
    ratios,
    wide,
    sem,
):
    copy = pltpu.make_async_copy(wide_hbm, wide, sem)
    copy.start()
    row = rows_of()
    lane = lanes_of()
    gx = lax.axis_index("gx")
    even = lax.rem(gx, 2) == 0
    west_in = (gx > 0).astype(F32)
    east_in = (gx < 7).astype(F32)

    def both(ref_a, ref_b, at, size):
        at = pl.multiple_of(at, 8)
        from_a = ref_a[pl.ds(at, size), :]
        from_b = ref_b[pl.ds(at, size), :]
        return jnp.where(even, from_b, from_a), jnp.where(even, from_a, from_b)

    def bring(d, _):
        for f in range(12):
            homes = both(side_a, side_b, (d * 12 + f) * 8, 8)
            souths = both(corner_a, corner_b, (d * 12 + f) * 16, 8)
            norths = both(corner_a, corner_b, (d * 12 + f) * 16 + 8, 8)
            for side, inside in ((0, west_in), (1, east_in)):
                here = d if side == 0 else 8 + EARLY + d
                for t, tiles in enumerate((souths, homes, norths)):
                    part = slice(8 * t, 8 * t + 8)
                    if f < NC:
                        iters[here, f, part, :] = tiles[side]
                    else:
                        perms[here, f - 9, part, :] = tiles[side] * inside
        return 0

    lax.fori_loop(0, EARLY, bring, 0)

    def bring_ratio(d, _):
        for c in range(NC):
            homes = both(side_a, side_b, SIDE_RATIO + (d * NC + c) * 8, 8)
            outers = both(corner_a, corner_b, CORNER_RATIO + (d * NC + c) * 8, 8)
            for side in range(2):
                here = d if side == 0 else LATE + d
                ratios[here, c, 0:8, :] = homes[side]
                ratios[here, c, 8:16, :] = outers[side]
        return 0

    lax.fori_loop(0, LATE, bring_ratio, 0)
    copy.wait()

    def settle(x, _):
        for f in range(NC):
            iters[EARLY + x, f] = wide[x, f]
        for f in range(3):
            perms[EARLY + x, f] = wide[x, 9 + f]
        return 0

    lax.fori_loop(0, 8, settle, 0)

    def column(at, ratio_of):
        here = at + 1

        def three(ref, *index):
            return tuple(ref[index + (slice(8 * t, 8 * t + 8), slice(None))] for t in range(3))

        px = three(perms, here, 0)
        py = three(perms, here, 1)
        pz = three(perms, here, 2)
        t_east = [a * b for a, b in zip(px, three(perms, here + 1, 0))]
        t_west = [a * b for a, b in zip(px, three(perms, here - 1, 0))]
        t_north = [a * b for a, b in zip(py, north_of(py, row))]
        t_south = [a * b for a, b in zip(py, south_of(py, row))]
        t_up = [jnp.where(lane < 127, a * pltpu.roll(a, 127, 1), 0.0) for a in pz]
        t_down = [jnp.where(lane > 0, a * pltpu.roll(a, 1, 1), 0.0) for a in pz]
        kinds = (t_east, t_west, t_north, t_south, t_up, t_down)
        total = [sum(kind[t] for kind in kinds) for t in range(3)]

        def outer(tiles):
            return jnp.where(row < 4, tiles[2], tiles[0])

        def edge(tiles):
            return jnp.where(row == 4, tiles[2], tiles[0])

        for n, kind in enumerate(kinds):
            trans[at, n, 0:8, :] = kind[1]
            trans[at, n, 8:16, :] = outer(kind)
        for c in range(NC):
            mid = three(iters, here, c)
            east = three(iters, here + 1, c)
            west = three(iters, here - 1, c)
            north = north_of(mid, row)
            south = south_of(mid, row)
            beside = []
            for t in range(3):
                value = t_east[t] * east[t] + t_west[t] * west[t]
                value = value + t_north[t] * north[t] + t_south[t] * south[t]
                value = value + t_up[t] * pltpu.roll(mid[t], 127, 1)
                value = value + t_down[t] * pltpu.roll(mid[t], 1, 1)
                beside.append(value)
            ratio = ratio_of(c)
            scale = OMEGA / (ratio[0] + total[1])
            gain[at, c, 0:8, :] = scale
            begin[at, c, 0:8, :] = KEEP * mid[1] + scale * beside[1]
            scale = OMEGA / (ratio[1] + outer(total))
            gain[at, c, 8:16, :] = scale
            begin[at, c, 8:16, :] = KEEP * outer(mid) + scale * outer(beside)
            if ratio[2] is not None:
                scale = OMEGA / (ratio[2] + edge(total))
                begin_edge[at - LATE, c] = KEEP * edge(mid) + scale * edge(beside)

    def home_column(x, _):
        def ratio_of(c):
            south = wide[x, 12 + c, 0:8, :]
            north = wide[x, 12 + c, 16:24, :]
            return (
                wide[x, 12 + c, 8:16, :],
                jnp.where(row < 4, north, south),
                jnp.where(row == 4, north, south),
            )

        column(x + LATE, ratio_of)
        return 0

    def halo_column(d, _):
        def ratio_of(c):
            return (ratios[d, c, 0:8, :], ratios[d, c, 8:16, :], None)

        column(jnp.where(d < LATE, d, d + 8), ratio_of)
        return 0

    lax.fori_loop(0, 8, home_column, 0)
    lax.fori_loop(0, 2 * LATE, halo_column, 0)


def scatter_kernel(
    cell,
    arrived,
    scale_hbm,
    base_hbm,
    weight,
    send_a,
    send_b,
    side_a,
    side_b,
    left,
    right,
    scale,
    base,
    sems,
):
    copies = fetch(
        (scale_hbm, base_hbm),
        (scale, base),
        sems,
    )
    row16 = rows_of((16, 128))

    def mark(j, _):
        for half in range(2):
            at = pl.ds(pl.multiple_of(j * 256 + half * 128, 128), 128)
            place = jnp.broadcast_to(cell[j, half : half + 1, :], (16, 128))
            high = lax.bitwise_or(
                lax.bitwise_and(place, 127),
                lax.shift_left(lax.shift_right_logical(place, 11), 7),
            )
            for n in range(32):
                right[n * 16 : n * 16 + 16, at] = jnp.where(
                    high == row16 + n * 16, 1.0, 0.0
                ).astype(BF16)
        return 0

    lax.fori_loop(0, BRICKS, mark, 0)
    def build(j, _):
        for half in range(2):
            at = pl.ds(pl.multiple_of(j * 256 + half * 128, 128), 128)
            place = cell[j, half : half + 1, :]
            place = jnp.broadcast_to(place, (16, 128))
            low = lax.bitwise_and(lax.shift_right_logical(place, 7), 15)
            mine = low == row16
            values = arrived[j, pl.ds(half, NC, stride=2), :]
            coarse = values.astype(BF16).astype(F32)
            fine = values - coarse
            for c in range(NC):
                for part, source in ((0, coarse), (1, fine)):
                    line = jnp.broadcast_to(source[c : c + 1, :], (16, 128))
                    left[part * 144 + c * 16 : part * 144 + c * 16 + 16, at] = jnp.where(
                        mine, line, 0.0
                    ).astype(BF16)
        return 0

    lax.fori_loop(0, BRICKS, build, 0)

    for part in range(2):
        if part == 0:
            copies[0].wait()
            copies[1].wait()
        product = lax.dot_general(
            left[...],
            right[part * 256 : part * 256 + 256, :],
            (((1,), (1,)), ((), ())),
            preferred_element_type=F32,
        )
        for side in range(2):
            pair = part * 2 + side
            at = slice(side * 128, side * 128 + 128)
            for c in range(NC):
                well = product[c * 16 : c * 16 + 16, at] + product[144 + c * 16 : 160 + c * 16, at]
                here = slice((c * 4 + pair) * 16, (c * 4 + pair) * 16 + 16)
                weight[here, :] = base[here, :] - scale[here, :] * well

    even = lax.rem(lax.axis_index("gy"), 2) == 0
    for buffer in (send_a, send_b):
        buffer[0:8, :] = jnp.zeros(TILE, F32)
        buffer[LATE_ROWS - 8 : LATE_ROWS, :] = jnp.zeros(TILE, F32)
    for i in range(NC * 8):
        low = weight[i * 8 : i * 8 + LATE, :]
        high = weight[i * 8 + 8 - LATE : i * 8 + 8, :]
        at = slice(8 + i * LATE, 8 + i * LATE + LATE)
        send_a[at, :] = jnp.where(even, high, low)
        send_b[at, :] = jnp.where(even, low, high)
    even_x = lax.rem(lax.axis_index("gx"), 2) == 0
    for buffer, east in ((side_a, even_x), (side_b, jnp.logical_not(even_x))):
        first = jnp.where(east, 8 - LATE, 0)
        for d in range(LATE):
            for c in range(NC):
                at = pl.multiple_of((c * 8 + d + first) * 8, 8)
                buffer[d, c] = weight[pl.ds(at, 8), :]


def late_wide_kernel(weight, recv_a, recv_b, wide, edge, send_a, send_b):
    row = rows_of()
    even = lax.rem(lax.axis_index("gy"), 2) == 0
    for c in range(NC):
        for x in range(8):
            i = c * 8 + x
            at = 8 + i * LATE
            low = slice(at - (8 - LATE), at + LATE)
            high = slice(at, at + 8)
            south = jnp.where(even, recv_b[low, :], recv_a[low, :])
            north = jnp.where(even, recv_a[high, :], recv_b[high, :])
            wide[x, c, 0:8, :] = weight[i * 8 : i * 8 + 8, :]
            wide[x, c, 8:16, :] = jnp.where(row < 4, north, south)
            edge[x, c] = jnp.where(row == 4, north, south)
    even_x = lax.rem(lax.axis_index("gx"), 2) == 0
    for buffer, east in ((send_a, even_x), (send_b, jnp.logical_not(even_x))):
        first = jnp.where(east, 8 - LATE, 0)
        for d in range(LATE):
            for c in range(NC):
                buffer[d, c] = wide[first + d, c, 8:16, :]


def sweep_kernel(
    trans,
    gain,
    begin,
    begin_edge,
    wide,
    edge,
    side_a,
    side_b,
    corner_a,
    corner_b,
    result,
    weight,
    one,
    two,
    last_one,
    sems,
):
    row = rows_of()
    even = lax.rem(lax.axis_index("gx"), 2) == 0

    def bring(d, _):
        for c in range(NC):
            for t, (ref_a, ref_b) in enumerate(((side_a, side_b), (corner_a, corner_b))):
                part = slice(8 * t, 8 * t + 8)
                west = jnp.where(even, ref_b[d, c], ref_a[d, c])
                east = jnp.where(even, ref_a[d, c], ref_b[d, c])
                weight[d, c, part, :] = west
                weight[8 + LATE + d, c, part, :] = east
                one[d, c, part, :] = west + begin[d, c, part, :]
                one[8 + LATE + d, c, part, :] = east + begin[8 + LATE + d, c, part, :]
        return 0

    lax.fori_loop(0, LATE, bring, 0)

    def settle(x, _):
        for c in range(NC):
            weight[LATE + x, c] = wide[x, c]
            one[LATE + x, c] = wide[x, c] + begin[LATE + x, c]
        return 0

    lax.fori_loop(0, 8, settle, 0)
    first = row == 0
    last = row == 7

    def column(at, held, new, brim, final):
        kinds = [[trans[at, n, 8 * t : 8 * t + 8, :] for t in range(2)] for n in range(6)]
        t_east, t_west, t_north, t_south, t_up, t_down = kinds
        for c in range(NC):
            mid = [held[at, c, 8 * t : 8 * t + 8, :] for t in range(2)]
            east = [held[at + 1, c, 8 * t : 8 * t + 8, :] for t in range(2)]
            west = [held[at - 1, c, 8 * t : 8 * t + 8, :] for t in range(2)]
            back = [pltpu.roll(tile, 7, 0) for tile in mid]
            fore = [pltpu.roll(tile, 1, 0) for tile in mid]
            north = [jnp.where(last, back[1], back[0]), jnp.where(last, back[0], back[1])]
            south = [jnp.where(first, fore[1], fore[0]), jnp.where(first, fore[0], fore[1])]
            if brim:
                outer = begin_edge[at - LATE, c] + edge[at - LATE, c]
                north[1] = jnp.where(row == 3, pltpu.roll(outer, 7, 0), north[1])
                south[1] = jnp.where(row == 4, pltpu.roll(outer, 1, 0), south[1])
            for t in range(1 if final else 2):
                value = t_east[t] * east[t] + t_west[t] * west[t]
                value = value + t_north[t] * north[t] + t_south[t] * south[t]
                value = value + t_up[t] * pltpu.roll(mid[t], 127, 1)
                value = value + t_down[t] * pltpu.roll(mid[t], 1, 1)
                part = slice(8 * t, 8 * t + 8)
                value = KEEP * mid[t] + weight[at, c, part, :] + gain[at, c, part, :] * value
                if final:
                    last_one[at - LATE, c] = value
                else:
                    new[at, c, part, :] = value

    def writing(x):
        return pltpu.make_async_copy(last_one.at[x], result.at[:, x], sems.at[x])

    def sweep(begin_at, end_at, held, new, brim=False, final=False):
        count = end_at - begin_at
        whole = count // 8 * 8

        def run(at, size):
            for step in range(size):
                column(at + step, held, new, brim, final)
                if final:
                    writing(at + step - LATE).start()
            return 0

        if whole:
            lax.fori_loop(0, whole // 8, lambda i, _: run(begin_at + i * 8, 8), 0)
        if count > whole:
            lax.fori_loop(0, 1, lambda i, _: run(begin_at + whole + i, count - whole), 0)

    sweep(1, LATE, one, two)
    sweep(LATE, LATE + 8, one, two, brim=True)
    sweep(LATE + 8, COLS - 1, one, two)
    sweep(2, COLS - 2, two, one)
    sweep(3, COLS - 3, one, two)
    sweep(4, COLS - 4, two, one)
    sweep(5, COLS - 5, one, None, final=True)
    for x in range(8):
        writing(x).wait()


def swap_pairs(shards, axis):
    axes = ("gx", "gy")
    sizes = [lax.axis_size(name) for name in axes]
    along = axes.index(axis)
    inner, outer = [], []
    for i in range(sizes[0]):
        for j in range(sizes[1]):
            place = [i, j]
            near, far_one = list(place), list(place)
            near[along] = place[along] ^ 1
            if along == 0 or 0 < place[1] < sizes[1] - 1:
                far_one[along] = (((place[along] + 1) ^ 1) - 1) % sizes[along]
            else:
                far_one[0] = i ^ 1
            here = i * sizes[1] + j
            inner.append((here, near[0] * sizes[1] + near[1]))
            outer.append((here, far_one[0] * sizes[1] + far_one[1]))
    return lax.ppermute(shards[0], axes, inner), lax.ppermute(shards[1], axes, outer)


def body(
    seg_source,
    seg_inverse,
    seg_outflow,
    well_len,
    perf_seg,
    perf_count,
    perf_coupling,
    recv_cell,
    cell_cot,
    start_iterate,
    accumulation,
    mobility,
    perm_x,
    perm_y,
    perm_z,
):
    cot = cell_cot.reshape(NC * 64, 128)
    accum = accumulation.reshape(NC * 64, 128)
    mobil = mobility.reshape(NC * 64, 128)
    held = [
        pltpu.VMEM((NC, 8, 8, 128), F32),
        pltpu.VMEM((8, 8, 128), F32),
        pltpu.VMEM((8, 8, 128), F32),
        pltpu.VMEM((8, 8, 128), F32),
        pltpu.VMEM((NC * 64, 128), BF16),
        pltpu.VMEM((NC * 64, 128), BF16),
    ]
    given = [pin(x) for x in (start_iterate, perm_x, perm_y, perm_z, accum, mobil)]
    mats, vecs, head, ratio, early_a, early_b, side_a, side_b = call(
        first_kernel,
        (
            out(81, 8, 128),
            out(NC, 8, 128),
            far(BRICKS, 8, 128),
            out(NC * 64, 128),
            far(EARLY_ROWS, 128),
            far(EARLY_ROWS, 128),
            far(SIDE_ROWS, 128),
            far(SIDE_ROWS, 128),
        ),
        [
            pltpu.VMEM((90, 8, 128), F32),
            pltpu.VMEM((BRICKS, 8, 128), F32),
            pltpu.VMEM((EARLY_ROWS, 128), F32),
            pltpu.VMEM((EARLY_ROWS, 128), F32),
            pltpu.VMEM((SIDE_ROWS, 128), F32),
            pltpu.VMEM((SIDE_ROWS, 128), F32),
            pltpu.SMEM((8,), I32),
            pltpu.VMEM((NC, 8, 128), F32),
            pltpu.VMEM((NC, NC, 8, 128), F32),
            pltpu.VMEM((NC, NC, 8, 128), F32),
        ]
        + held
        + [pltpu.SemaphoreType.DMA((10,)), pltpu.SemaphoreType.DMA((5,))],
        [HBM] * 10,
        "first",
        10_000_000,
        out_specs=(VMEM, VMEM, HBM, VMEM, HBM, HBM, HBM, HBM),
    )(pin(well_len), pin(seg_source), pin(seg_inverse), pin(seg_outflow), *given)
    heads = lax.all_to_all(head, "gy", 0, 0, tiled=True)
    early_a, early_b = swap_pairs((early_a, early_b), "gy")

    side_a, side_b = swap_pairs((side_a, side_b), "gx")
    lam, sent, token = call(
        rows_kernel,
        (
            far(NC, 8, 128),
            far(BRICKS * SLOT, 128),
            out(8, 128),
        ),
        [
            pltpu.VMEM((NC, 8, 128), F32),
            pltpu.VMEM((BRICKS * SLOT, 128), F32),
            pltpu.SMEM((BRICKS,), I32),
            pltpu.VMEM((BRICKS, 256), I32),
            pltpu.VMEM((NC, NC, BRICKS, 256), F32),
            pltpu.SemaphoreType.DMA,
            pltpu.SemaphoreType.DMA((3,)),
            pltpu.SemaphoreType.DMA((2,)),
        ],
        [HBM] * 3 + [VMEM] * 3,
        "well_rows",
        20_000_000_000,
        out_specs=(HBM, HBM, VMEM),
    )(
        pin(perf_count.reshape(BRICKS)),
        pin(perf_seg.reshape(BRICKS, 256)),
        pin(perf_coupling.reshape(NC, NC, BRICKS, 256)),
        mats,
        vecs,
        heads,
    )
    arrived = lax.all_to_all(sent, "gy", 0, 0, tiled=True)

    cell = recv_cell.reshape(BRICKS, 2, 128)
    wide, corner_a, corner_b, scale, base = call(
        shade_kernel,
        (
            far(8, FIELDS, 24, 128),
            far(CORNER_ROWS, 128),
            far(CORNER_ROWS, 128),
            far(NC * 64, 128),
            far(NC * 64, 128),
        ),
        held
        + [
            pltpu.VMEM((NC * 64, 128), BF16),
            pltpu.VMEM((8, FIELDS, 24, 128), F32),
            pltpu.VMEM((CORNER_ROWS, 128), F32),
            pltpu.VMEM((CORNER_ROWS, 128), F32),
            pltpu.VMEM((NC * 64, 128), F32),
            pltpu.VMEM((NC * 64, 128), F32),
            pltpu.SemaphoreType.DMA((7,)),
            pltpu.SemaphoreType.DMA((5,)),
        ],
        [VMEM] + [HBM] * 7 + [VMEM] * 5,
        "shade",
        limit=12,
        out_specs=(HBM,) * 5,
    )(token, *given, pin(cot), ratio, early_a, early_b, side_a, side_b)
    corner_a, corner_b = swap_pairs((corner_a, corner_b), "gx")

    weight, late_a, late_b, late_side_a, late_side_b = call(
        scatter_kernel,
        (
            out(NC * 64, 128),
            out(LATE_ROWS, 128),
            out(LATE_ROWS, 128),
            out(LATE, NC, 8, 128),
            out(LATE, NC, 8, 128),
        ),
        [
            pltpu.VMEM((288, 4096), BF16),
            pltpu.VMEM((512, 4096), BF16),
            pltpu.VMEM((NC * 64, 128), F32),
            pltpu.VMEM((NC * 64, 128), F32),
            pltpu.SemaphoreType.DMA((2,)),
        ],
        [VMEM] * 2 + [HBM] * 2,
        "scatter",
        20_000_000_000,
        limit=16,
    )(cell, arrived.reshape(BRICKS, SLOT, 128), pin(scale), pin(base))
    late_a, late_b = swap_pairs((late_a, late_b), "gy")
    late_side_a, late_side_b = swap_pairs((late_side_a, late_side_b), "gx")

    trans, gain, begin, begin_edge = call(
        early_kernel,
        (
            out(COLS, 6, 16, 128),
            out(COLS, NC, 16, 128),
            out(COLS, NC, 16, 128),
            out(8, NC, 8, 128),
        ),
        [
            pltpu.VMEM((8 + 2 * EARLY, NC, 24, 128), F32),
            pltpu.VMEM((8 + 2 * EARLY, 3, 24, 128), F32),
            pltpu.VMEM((2 * LATE, NC, 16, 128), F32),
            pltpu.VMEM((8, FIELDS, 24, 128), F32),
            pltpu.SemaphoreType.DMA,
        ],
        [HBM] + [VMEM] * 4,
        "early",
        limit=10,
    )(pin(wide), side_a, side_b, corner_a, corner_b)

    widened, edge, late_corner_a, late_corner_b = call(
        late_wide_kernel,
        (
            out(8, NC, 16, 128),
            out(8, NC, 8, 128),
            out(LATE, NC, 8, 128),
            out(LATE, NC, 8, 128),
        ),
        [],
        [VMEM] * 3,
        "late_wide",
    )(weight, late_a, late_b)
    late_corner_a, late_corner_b = swap_pairs((late_corner_a, late_corner_b), "gx")

    wide_field = pltpu.VMEM((COLS, NC, 16, 128), F32)
    result = call(
        sweep_kernel,
        out(NC, 8, 8, 128),
        [wide_field] * 3
        + [pltpu.VMEM((8, NC, 8, 128), F32), pltpu.SemaphoreType.DMA((8,))],
        [VMEM] * 10,
        "sweeps",
        out_specs=HBM,
    )(
        trans,
        gain,
        begin,
        begin_edge,
        widened,
        edge,
        late_side_a,
        late_side_b,
        late_corner_a,
        late_corner_b,
    )
    return lam, result


def solution(mesh):
    return jax.shard_map(
        body,
        mesh=mesh,
        in_specs=(
            P(None, "gx", "gy"),
            P(None, None, "gx", "gy"),
            P(None, None, "gx", "gy"),
            P("gx"),
            P("gx", "gy", None, None),
            P("gx", "gy", None),
            P(None, None, "gx", "gy", None, None),
            P("gx", "gy", None, None),
            P(None, "gx", "gy", None),
            P(None, "gx", "gy", None),
            P(None, "gx", "gy", None),
            P(None, "gx", "gy", None),
            P("gx", "gy", None),
            P("gx", "gy", None),
            P("gx", "gy", None),
        ),
        out_specs=(P(None, "gx", "gy"), P(None, "gx", "gy", None)),
        check_vma=False,
    )
```

```python
import jax
import jax.numpy as jnp
from jax import lax
from jax.experimental import pallas as pl
from jax.experimental.pallas import tpu as pltpu
from jax.sharding import PartitionSpec as P

F32 = jnp.float32
BF16 = jnp.bfloat16
I32 = jnp.int32
NC = 9
OMEGA = 0.8
KEEP = 1.0 - OMEGA
BRICKS = 16
EARLY = 6
LATE = 5
TILE = (8, 128)
FIELDS = 21
EARLY_ROWS = 16 + FIELDS * 8 * EARLY
LATE_ROWS = 16 + NC * 8 * LATE
SIDE_RATIO = 12 * EARLY * 8
SIDE_ROWS = SIDE_RATIO + NC * LATE * 8
CORNER_RATIO = 12 * EARLY * 16
CORNER_ROWS = CORNER_RATIO + NC * LATE * 8
COLS = 8 + 2 * LATE
SLOT = 24
CHUNKS = 4

VMEM = pl.BlockSpec(memory_space=pltpu.VMEM)
SMEM = pl.BlockSpec(memory_space=pltpu.SMEM)
HBM = pl.BlockSpec(memory_space=pltpu.HBM)


def lanes_of(shape=TILE):
    return lax.broadcasted_iota(I32, shape, 1)


def rows_of(shape=TILE):
    return lax.broadcasted_iota(I32, shape, 0)


def call(kernel, outs, scratch, specs, name, flops=1_000_000, limit=8, out_specs=None):
    return pl.pallas_call(
        kernel,
        out_shape=outs,
        in_specs=specs,
        out_specs=jax.tree.map(lambda _: VMEM, outs) if out_specs is None else out_specs,
        scratch_shapes=scratch,
        compiler_params=pltpu.CompilerParams(vmem_limit_bytes=limit * 1024 * 1024),
        cost_estimate=pl.CostEstimate(
            flops=flops, bytes_accessed=1_000_000, transcendentals=0
        ),
        name=name,
    )


def out(*shape, dtype=F32):
    return jax.ShapeDtypeStruct(shape, dtype)


def far(*shape, dtype=F32):
    return pltpu.HBM(shape, dtype)


def pin(array):
    return pltpu.with_memory_space_constraint(array, pltpu.HBM)


def fetch(sources, targets, sems):
    copies = [
        pltpu.make_async_copy(source, target, sems.at[n])
        for n, (source, target) in enumerate(zip(sources, targets))
    ]
    for copy in copies:
        copy.start()
    return copies


def first_kernel(
    len_hbm,
    src_hbm,
    inv_hbm,
    outf_hbm,
    start_hbm,
    px_hbm,
    py_hbm,
    pz_hbm,
    accum_hbm,
    mobil_hbm,
    mats,
    vecs,
    head_hbm,
    ratio,
    send_a_hbm,
    send_b_hbm,
    side_a_hbm,
    side_b_hbm,
    rolled,
    head,
    send_a,
    send_b,
    side_a,
    side_b,
    len_ref,
    src,
    inv,
    outf,
    start,
    px,
    py,
    pz,
    accum,
    mobil,
    sems,
    sems_out,
):
    copies = fetch(
        (
            inv_hbm,
            outf_hbm,
            src_hbm,
            len_hbm,
            start_hbm,
            px_hbm,
            py_hbm,
            pz_hbm,
            accum_hbm,
            mobil_hbm,
        ),
        (inv, outf, src, len_ref, start, px, py, pz, accum, mobil),
        sems,
    )
    for copy in copies[4:]:
        copy.wait()
    early_pack(start, px, py, pz, accum, mobil, ratio, send_a, send_b, side_a, side_b)
    moves = fetch(
        (send_a, send_b, side_a, side_b),
        (send_a_hbm, send_b_hbm, side_a_hbm, side_b_hbm),
        sems_out,
    )
    for copy in copies[:4]:
        copy.wait()
    scan_wells(len_ref, src, inv, outf, mats, vecs, head, rolled)
    moves.append(pltpu.make_async_copy(head, head_hbm, sems_out.at[4]))
    moves[-1].start()
    for move in moves:
        move.wait()


def scan_wells(len_ref, src, inv, outf, mats, vecs, head, rolled):
    lane = lanes_of()
    well = rows_of()
    length = jnp.zeros(TILE, I32)
    for w in range(8):
        length = jnp.where(well == w, len_ref[w], length)
    active = (lax.axis_index("gy") * 128 + lane < length).astype(F32)

    def start(c, _):
        row = [inv[j, c] for j in range(NC)]
        total = row[0] * src[0]
        for j in range(1, NC):
            total = total + row[j] * src[j]
        vecs[c] = active * total
        for k in range(NC):
            total = row[0] * outf[k, 0]
            for j in range(1, NC):
                total = total + row[j] * outf[k, j]
            mats[c * NC + k] = -active * total
        return 0

    def starts(group, _):
        for a in range(3):
            start(group * 3 + a, 0)
        return 0

    lax.fori_loop(0, 3, starts, 0)

    def step(i, _):
        gap = lax.shift_left(jnp.int32(1), i)
        keep = lane < 128 - gap
        for k in range(NC):
            for m in range(NC):
                moved = pltpu.roll(mats[k * NC + m], 128 - gap, 1)
                rolled[k * 10 + m] = jnp.where(keep, moved, 1.0 if k == m else 0.0)
            rolled[k * 10 + 9] = jnp.where(keep, pltpu.roll(vecs[k], 128 - gap, 1), 0.0)

        def rows(group, _):
            rows3 = [[mats[(group * 3 + a) * NC + k] for k in range(NC)] for a in range(3)]
            for m in range(10):
                right = [rolled[k * 10 + m] for k in range(NC)]
                for a in range(3):
                    total = rows3[a][0] * right[0]
                    for k in range(1, NC):
                        total = total + rows3[a][k] * right[k]
                    if m < NC:
                        mats[(group * 3 + a) * NC + m] = total
                    else:
                        vecs[group * 3 + a] = vecs[group * 3 + a] + total
            return 0

        for group in range(3):
            rows(group, 0)
        return 0

    lax.fori_loop(0, 7, step, 0)
    packed = jnp.zeros(TILE, F32)
    for e in range(81):
        moved = mats[e] if e == 0 else pltpu.roll(mats[e], e, 1)
        packed = jnp.where(lane == e, moved, packed)
    for c in range(NC):
        packed = jnp.where(lane == 81 + c, pltpu.roll(vecs[c], 81 + c, 1), packed)
    for j in range(BRICKS):
        head[j] = packed


def rows_kernel(
    count_hbm,
    seg_hbm,
    coupling_hbm,
    mats,
    vecs,
    heads,
    lam_hbm,
    sent_hbm,
    token,
    lam,
    sent,
    count_ref,
    perf_seg,
    coupling,
    sem,
    sems,
    sems_out,
):
    copies = fetch(
        (count_hbm, seg_hbm, coupling_hbm), (count_ref, perf_seg, coupling), sems
    )
    row = rows_of()
    lane = lanes_of()
    me = lax.axis_index("gy")

    def hop(j, incoming):
        head = heads[j]
        later = j > me
        after = []
        for c in range(NC):
            total = jnp.broadcast_to(head[:, 81 + c : 82 + c], TILE)
            for k in range(NC):
                at = c * NC + k
                total = total + jnp.broadcast_to(head[:, at : at + 1], TILE) * incoming[k]
            after.append(total)
        return tuple(jnp.where(later, new, old) for new, old in zip(after, incoming))

    def hops(t, incoming):
        for step in range(5):
            incoming = hop(BRICKS - 1 - t * 5 - step, incoming)
        return incoming

    incoming = tuple(jnp.zeros(TILE, F32) for _ in range(NC))
    incoming = lax.fori_loop(0, 3, hops, incoming)
    for c in range(NC):
        total = vecs[c]
        for k in range(NC):
            total = total + mats[c * NC + k] * incoming[k]
        lam[c] = total
    moves = [pltpu.make_async_copy(lam, lam_hbm, sem)]
    moves[0].start()
    token[...] = jnp.zeros(TILE, F32)
    copies[0].wait()
    copies[1].wait()
    for block in range(2):
        count = jnp.zeros(TILE, I32)
        for b in range(8):
            count = jnp.where(row == b, count_ref[block * 8 + b], count)
        for half in range(2):
            at = (slice(block * 8, block * 8 + 8), slice(half * 128, half * 128 + 128))
            slot = perf_seg[at]
            slot_well = lax.shift_right_logical(slot, 7)
            slot_lane = lax.bitwise_and(slot, 127)
            is_well = [slot_well == w for w in range(8)]
            picked = []
            for k in range(NC):
                total = jnp.zeros(TILE, F32)
                for w in range(8):
                    line = jnp.broadcast_to(lam[k, w : w + 1, :], TILE)
                    got = jnp.take_along_axis(line, slot_lane, axis=1)
                    total = jnp.where(is_well[w], got, total)
                picked.append(total)
            live = lane + half * 128 < count
            if block == 0 and half == 0:
                copies[2].wait()
            for c in range(NC):
                total = coupling[(0, c) + at] * picked[0]
                for k in range(1, NC):
                    total = total + coupling[(k, c) + at] * picked[k]
                total = jnp.where(live, total, 0.0)
                sent[pl.ds(block * 8 * SLOT + c * 2 + half, 8, stride=SLOT), :] = total
        part = slice(block * 8 * SLOT, block * 8 * SLOT + 8 * SLOT)
        moves.append(
            pltpu.make_async_copy(sent.at[part], sent_hbm.at[part], sems_out.at[block])
        )
        moves[-1].start()
    for move in moves:
        move.wait()


def early_pack(start, px, py, pz, accum, mobil, ratio, send_a, send_b, side_a, side_b):
    even = lax.rem(lax.axis_index("gy"), 2) == 0
    for i in range(NC * 4):
        at = slice(i * 16, i * 16 + 16)
        ratio[at, :] = accum[at, :].astype(F32) / mobil[at, :].astype(F32)
    for buffer in (send_a, send_b):
        buffer[0:8, :] = jnp.zeros(TILE, F32)
        buffer[EARLY_ROWS - 8 : EARLY_ROWS, :] = jnp.zeros(TILE, F32)
    perms = (px, py, pz)
    for f in range(FIELDS):
        for x in range(8):
            if f < NC:
                low, high = start[f, x, 0:EARLY, :], start[f, x, 8 - EARLY : 8, :]
            elif f < 12:
                low, high = perms[f - 9][x, 0:EARLY, :], perms[f - 9][x, 8 - EARLY : 8, :]
            else:
                base = ((f - 12) * 8 + x) * 8
                low, high = ratio[base : base + EARLY, :], ratio[base + 8 - EARLY : base + 8, :]
            at = 8 + (f * 8 + x) * EARLY
            send_a[at : at + EARLY, :] = jnp.where(even, high, low)
            send_b[at : at + EARLY, :] = jnp.where(even, low, high)
    even_x = lax.rem(lax.axis_index("gx"), 2) == 0
    for buffer, east in ((side_a, even_x), (side_b, jnp.logical_not(even_x))):
        first = jnp.where(east, 8 - EARLY, 0)
        for d in range(EARLY):
            for f in range(12):
                at = (d * 12 + f) * 8
                tile = start[f, first + d] if f < NC else perms[f - 9][first + d]
                buffer[at : at + 8, :] = tile
        first = jnp.where(east, 8 - LATE, 0)
        for d in range(LATE):
            for c in range(NC):
                at = SIDE_RATIO + (d * NC + c) * 8
                base = pl.multiple_of((c * 8 + d + first) * 8, 8)
                buffer[at : at + 8, :] = ratio[pl.ds(base, 8), :]


def shade_kernel(
    after,
    start_hbm,
    px_hbm,
    py_hbm,
    pz_hbm,
    accum_hbm,
    mobil_hbm,
    cot_hbm,
    ratio,
    recv_a,
    recv_b,
    side_a,
    side_b,
    wide_hbm,
    send_a_hbm,
    send_b_hbm,
    scale_hbm,
    base_hbm,
    start,
    px,
    py,
    pz,
    accum,
    mobil,
    cot,
    wide,
    send_a,
    send_b,
    scale,
    base,
    sems,
    sems_out,
):
    copies = fetch(
        (start_hbm, px_hbm, py_hbm, pz_hbm, accum_hbm, mobil_hbm, cot_hbm),
        (start, px, py, pz, accum, mobil, cot),
        sems,
    )
    for copy in copies:
        copy.wait()
    row = rows_of()
    gy = lax.axis_index("gy")
    even = lax.rem(gy, 2) == 0
    south_in = (gy > 0).astype(F32)
    north_in = (gy < BRICKS - 1).astype(F32)
    perms = (px, py, pz)
    for f in range(FIELDS):
        for x in range(8):
            at = 8 + (f * 8 + x) * EARLY
            low = slice(at - (8 - EARLY), at + EARLY)
            high = slice(at, at + 8)
            south = jnp.where(even, recv_b[low, :], recv_a[low, :])
            north = jnp.where(even, recv_a[high, :], recv_b[high, :])
            if f < NC:
                home = start[f, x]
            elif f < 12:
                home = perms[f - 9][x]
                south = south * south_in
                north = north * north_in
            else:
                start_at = ((f - 12) * 8 + x) * 8
                home = ratio[start_at : start_at + 8, :]
            wide[x, f, 0:8, :] = south
            wide[x, f, 8:16, :] = home
            wide[x, f, 16:24, :] = north
    moves = fetch((wide,), (wide_hbm,), sems_out)
    even_x = lax.rem(lax.axis_index("gx"), 2) == 0
    for buffer, east in ((send_a, even_x), (send_b, jnp.logical_not(even_x))):
        first = jnp.where(east, 8 - EARLY, 0)
        for f in range(12):
            for d in range(EARLY):
                at = (d * 12 + f) * 16
                buffer[at : at + 8, :] = wide[first + d, f, 0:8, :]
                buffer[at + 8 : at + 16, :] = wide[first + d, f, 16:24, :]
        first = jnp.where(east, 8 - LATE, 0)
        for d in range(LATE):
            for c in range(NC):
                at = CORNER_RATIO + (d * NC + c) * 8
                buffer[at : at + 8, :] = jnp.where(
                    row < 4, wide[first + d, 12 + c, 16:24, :], wide[first + d, 12 + c, 0:8, :]
                )
    for n, (source, target) in enumerate(((send_a, send_a_hbm), (send_b, send_b_hbm))):
        moves.append(pltpu.make_async_copy(source, target, sems_out.at[1 + n]))
        moves[-1].start()
    gx = lax.axis_index("gx")
    west_at = slice(((EARLY - 1) * 12 + 9) * 8, ((EARLY - 1) * 12 + 10) * 8)
    east_at = slice(9 * 8, 10 * 8)
    px_west = jnp.where(even_x, side_b[west_at, :], side_a[west_at, :])
    px_west = px_west * (gx > 0).astype(F32)
    px_east = jnp.where(even_x, side_a[east_at, :], side_b[east_at, :])
    px_east = px_east * (gx < 7).astype(F32)
    lane = lanes_of()
    totals = []
    for x in range(8):
        east = px[x + 1] if x < 7 else px_east
        west = px[x - 1] if x > 0 else px_west
        value = px[x] * east + px[x] * west
        along = tuple(wide[x, 10, 8 * t : 8 * t + 8, :] for t in range(3))
        value = value + along[1] * north_of(along, row)[1] + along[1] * south_of(along, row)[1]
        value = value + jnp.where(lane < 127, pz[x] * pltpu.roll(pz[x], 127, 1), 0.0)
        value = value + jnp.where(lane > 0, pz[x] * pltpu.roll(pz[x], 1, 1), 0.0)
        totals.append(value)
    for pair in range(4):
        total = jnp.concatenate(totals[pair * 2 : pair * 2 + 2], axis=0)
        for c in range(NC):
            here = slice((c * 4 + pair) * 16, (c * 4 + pair) * 16 + 16)
            diagonal = accum[here, :].astype(F32) + mobil[here, :].astype(F32) * total
            inverse = OMEGA / diagonal
            scale[here, :] = inverse
            base[here, :] = inverse * cot[here, :].astype(F32)
    for n, (source, target) in enumerate(((scale, scale_hbm), (base, base_hbm))):
        moves.append(pltpu.make_async_copy(source, target, sems_out.at[3 + n]))
        moves[-1].start()
    for move in moves:
        move.wait()


def north_of(tiles, row):
    south, home, north = (pltpu.roll(tile, 7, 0) for tile in tiles)
    last = row == 7
    return (jnp.where(last, home, south), jnp.where(last, north, home), north)


def south_of(tiles, row):
    south, home, north = (pltpu.roll(tile, 1, 0) for tile in tiles)
    first = row == 0
    return (south, jnp.where(first, south, home), jnp.where(first, home, north))


def early_kernel(
    wide_hbm,
    side_a,
    side_b,
    corner_a,
    corner_b,
    trans,
    gain,
    begin,
    begin_edge,
    iters,
    perms,
    ratios,
    wide,
    sem,
):
    copy = pltpu.make_async_copy(wide_hbm, wide, sem)
    copy.start()
    row = rows_of()
    lane = lanes_of()
    gx = lax.axis_index("gx")
    even = lax.rem(gx, 2) == 0
    west_in = (gx > 0).astype(F32)
    east_in = (gx < 7).astype(F32)

    def both(ref_a, ref_b, at, size):
        at = pl.multiple_of(at, 8)
        from_a = ref_a[pl.ds(at, size), :]
        from_b = ref_b[pl.ds(at, size), :]
        return jnp.where(even, from_b, from_a), jnp.where(even, from_a, from_b)

    def bring(d, _):
        for f in range(12):
            homes = both(side_a, side_b, (d * 12 + f) * 8, 8)
            souths = both(corner_a, corner_b, (d * 12 + f) * 16, 8)
            norths = both(corner_a, corner_b, (d * 12 + f) * 16 + 8, 8)
            for side, inside in ((0, west_in), (1, east_in)):
                here = d if side == 0 else 8 + EARLY + d
                for t, tiles in enumerate((souths, homes, norths)):
                    part = slice(8 * t, 8 * t + 8)
                    if f < NC:
                        iters[here, f, part, :] = tiles[side]
                    else:
                        perms[here, f - 9, part, :] = tiles[side] * inside
        return 0

    lax.fori_loop(0, EARLY, bring, 0)

    def bring_ratio(d, _):
        for c in range(NC):
            homes = both(side_a, side_b, SIDE_RATIO + (d * NC + c) * 8, 8)
            outers = both(corner_a, corner_b, CORNER_RATIO + (d * NC + c) * 8, 8)
            for side in range(2):
                here = d if side == 0 else LATE + d
                ratios[here, c, 0:8, :] = homes[side]
                ratios[here, c, 8:16, :] = outers[side]
        return 0

    lax.fori_loop(0, LATE, bring_ratio, 0)
    copy.wait()

    def settle(x, _):
        for f in range(NC):
            iters[EARLY + x, f] = wide[x, f]
        for f in range(3):
            perms[EARLY + x, f] = wide[x, 9 + f]
        return 0

    lax.fori_loop(0, 8, settle, 0)

    def column(at, ratio_of):
        here = at + 1

        def three(ref, *index):
            return tuple(ref[index + (slice(8 * t, 8 * t + 8), slice(None))] for t in range(3))

        px = three(perms, here, 0)
        py = three(perms, here, 1)
        pz = three(perms, here, 2)
        t_east = [a * b for a, b in zip(px, three(perms, here + 1, 0))]
        t_west = [a * b for a, b in zip(px, three(perms, here - 1, 0))]
        t_north = [a * b for a, b in zip(py, north_of(py, row))]
        t_south = [a * b for a, b in zip(py, south_of(py, row))]
        t_up = [jnp.where(lane < 127, a * pltpu.roll(a, 127, 1), 0.0) for a in pz]
        t_down = [jnp.where(lane > 0, a * pltpu.roll(a, 1, 1), 0.0) for a in pz]
        kinds = (t_east, t_west, t_north, t_south, t_up, t_down)
        total = [sum(kind[t] for kind in kinds) for t in range(3)]

        def outer(tiles):
            return jnp.where(row < 4, tiles[2], tiles[0])

        def edge(tiles):
            return jnp.where(row == 4, tiles[2], tiles[0])

        for n, kind in enumerate(kinds):
            trans[at, n, 0:8, :] = kind[1]
            trans[at, n, 8:16, :] = outer(kind)
        for c in range(NC):
            mid = three(iters, here, c)
            east = three(iters, here + 1, c)
            west = three(iters, here - 1, c)
            north = north_of(mid, row)
            south = south_of(mid, row)
            beside = []
            for t in range(3):
                value = t_east[t] * east[t] + t_west[t] * west[t]
                value = value + t_north[t] * north[t] + t_south[t] * south[t]
                value = value + t_up[t] * pltpu.roll(mid[t], 127, 1)
                value = value + t_down[t] * pltpu.roll(mid[t], 1, 1)
                beside.append(value)
            ratio = ratio_of(c)
            scale = OMEGA / (ratio[0] + total[1])
            gain[at, c, 0:8, :] = scale
            begin[at, c, 0:8, :] = KEEP * mid[1] + scale * beside[1]
            scale = OMEGA / (ratio[1] + outer(total))
            gain[at, c, 8:16, :] = scale
            begin[at, c, 8:16, :] = KEEP * outer(mid) + scale * outer(beside)
            if ratio[2] is not None:
                scale = OMEGA / (ratio[2] + edge(total))
                begin_edge[at - LATE, c] = KEEP * edge(mid) + scale * edge(beside)

    def pairs(body):
        def run(i, _):
            body(i * 2, 0)
            return body(i * 2 + 1, 0)

        return run

    def home_column(x, _):
        def ratio_of(c):
            south = wide[x, 12 + c, 0:8, :]
            north = wide[x, 12 + c, 16:24, :]
            return (
                wide[x, 12 + c, 8:16, :],
                jnp.where(row < 4, north, south),
                jnp.where(row == 4, north, south),
            )

        column(x + LATE, ratio_of)
        return 0

    def halo_column(d, _):
        def ratio_of(c):
            return (ratios[d, c, 0:8, :], ratios[d, c, 8:16, :], None)

        column(jnp.where(d < LATE, d, d + 8), ratio_of)
        return 0

    lax.fori_loop(0, 4, pairs(home_column), 0)
    lax.fori_loop(0, LATE, pairs(halo_column), 0)


def scatter_kernel(
    cell,
    arrived,
    scale_hbm,
    base_hbm,
    weight,
    send_a,
    send_b,
    side_a,
    side_b,
    left_one,
    left_two,
    right_one,
    right_two,
    scale,
    base,
    sems,
):
    copies = fetch(
        (scale_hbm, base_hbm),
        (scale, base),
        sems,
    )
    row16 = rows_of((16, 128))

    row_mark = row16.astype(F32).astype(BF16)
    nothing = jnp.bfloat16(0.0)

    def mark(j, at_j, left, right):
        for half in range(2):
            at = slice(at_j * 256 + half * 128, at_j * 256 + half * 128 + 128)
            place = jnp.broadcast_to(cell[j, half : half + 1, :], (16, 128))
            block = lax.bitwise_or(
                lax.bitwise_and(lax.shift_right_logical(place, 4), 7),
                lax.shift_left(lax.shift_right_logical(place, 12), 3),
            )
            block = block.astype(F32).astype(BF16)
            mark16 = jnp.where(lax.bitwise_and(place, 15) == row16, 1.0, 0.0).astype(BF16)
            for n in range(16):
                right[n * 16 : n * 16 + 16, at] = jnp.where(
                    block == jnp.bfloat16(n), mark16, nothing
                )
            low = lax.bitwise_and(lax.shift_right_logical(place, 7), 31)
            low = low.astype(F32).astype(BF16)
            mine = (low == row_mark, low == row_mark + jnp.bfloat16(16))
            values = arrived[j, pl.ds(half, NC, stride=2), :]
            coarse = values.astype(BF16).astype(F32)
            fine = values - coarse
            for c in range(NC):
                for part, source in ((0, coarse), (1, fine)):
                    line = jnp.broadcast_to(source[c : c + 1, :], (16, 128)).astype(BF16)
                    for t in range(2):
                        first = part * 288 + c * 32 + t * 16
                        left[first : first + 16, at] = jnp.where(mine[t], line, nothing)

    size = BRICKS // CHUNKS
    lefts, rights = (left_one, left_two), (right_one, right_two)
    product = jnp.zeros((576, 256), F32)
    for chunk in range(CHUNKS + 1):
        if chunk < CHUNKS:
            for n in range(size):
                mark(chunk * size + n, n, lefts[chunk % 2], rights[chunk % 2])
        if chunk > 0:
            product = product + lax.dot_general(
                lefts[(chunk - 1) % 2][...],
                rights[(chunk - 1) % 2][...],
                (((1,), (1,)), ((), ())),
                preferred_element_type=F32,
            )
    for copy in copies:
        copy.wait()
    for c in range(NC):
        for side in range(2):
            at = slice(side * 128, side * 128 + 128)
            well = product[c * 32 : c * 32 + 32, at] + product[288 + c * 32 : 320 + c * 32, at]
            here = slice((c * 2 + side) * 32, (c * 2 + side) * 32 + 32)
            weight[here, :] = base[here, :] - scale[here, :] * well

    even = lax.rem(lax.axis_index("gy"), 2) == 0
    for buffer in (send_a, send_b):
        buffer[0:8, :] = jnp.zeros(TILE, F32)
        buffer[LATE_ROWS - 8 : LATE_ROWS, :] = jnp.zeros(TILE, F32)
    for i in range(NC * 8):
        low = weight[i * 8 : i * 8 + LATE, :]
        high = weight[i * 8 + 8 - LATE : i * 8 + 8, :]
        at = slice(8 + i * LATE, 8 + i * LATE + LATE)
        send_a[at, :] = jnp.where(even, high, low)
        send_b[at, :] = jnp.where(even, low, high)
    even_x = lax.rem(lax.axis_index("gx"), 2) == 0
    for buffer, east in ((side_a, even_x), (side_b, jnp.logical_not(even_x))):
        first = jnp.where(east, 8 - LATE, 0)
        for d in range(LATE):
            for c in range(NC):
                at = pl.multiple_of((c * 8 + d + first) * 8, 8)
                buffer[d, c] = weight[pl.ds(at, 8), :]


def late_wide_kernel(weight, recv_a, recv_b, wide, edge, send_a, send_b):
    row = rows_of()
    even = lax.rem(lax.axis_index("gy"), 2) == 0
    for c in range(NC):
        for x in range(8):
            i = c * 8 + x
            at = 8 + i * LATE
            low = slice(at - (8 - LATE), at + LATE)
            high = slice(at, at + 8)
            south = jnp.where(even, recv_b[low, :], recv_a[low, :])
            north = jnp.where(even, recv_a[high, :], recv_b[high, :])
            wide[x, c, 0:8, :] = weight[i * 8 : i * 8 + 8, :]
            wide[x, c, 8:16, :] = jnp.where(row < 4, north, south)
            edge[x, c] = jnp.where(row == 4, north, south)
    even_x = lax.rem(lax.axis_index("gx"), 2) == 0
    for buffer, east in ((send_a, even_x), (send_b, jnp.logical_not(even_x))):
        first, step = jnp.where(east, 7, 0), jnp.where(east, -1, 1)
        for c in range(NC):
            one, two, three, four = (wide[first + n * step, c, 8:16, :] for n in range(4))
            buffer[0, c] = one
            buffer[1, c] = jnp.where(
                row == 3,
                pltpu.roll(four, 3, 0),
                jnp.where(row == 4, pltpu.roll(four, 5, 0), two),
            )
            buffer[2, c] = three


def sweep_kernel(
    trans,
    gain,
    begin,
    begin_edge,
    wide,
    edge,
    side_a,
    side_b,
    corner_a,
    corner_b,
    result,
    weight,
    one,
    two,
    last_one,
    sems,
):
    row = rows_of()
    even = lax.rem(lax.axis_index("gx"), 2) == 0

    def place(at, c, part, tile):
        weight[at, c, part, :] = tile
        one[at, c, part, :] = tile + begin[at, c, part, :]

    def bring(c, _):
        home, outer = slice(0, 8), slice(8, 16)
        for d in range(LATE):
            place(d, c, home, jnp.where(even, side_b[d, c], side_a[d, c]))
            place(8 + LATE + d, c, home, jnp.where(even, side_a[d, c], side_b[d, c]))
        for near, ref_odd, ref_even in ((4, corner_a, corner_b), (13, corner_b, corner_a)):
            step = -1 if near == 4 else 1
            tiles = [jnp.where(even, ref_even[n, c], ref_odd[n, c]) for n in range(3)]
            far_tile = jnp.where(row == 0, pltpu.roll(tiles[1], 5, 0), pltpu.roll(tiles[1], 3, 0))
            for n, tile in enumerate((tiles[0], tiles[1], tiles[2], far_tile, far_tile)):
                place(near + n * step, c, outer, tile)
        return 0

    lax.fori_loop(0, NC, bring, 0)

    def settle(x, _):
        for c in range(NC):
            weight[LATE + x, c] = wide[x, c]
            one[LATE + x, c] = wide[x, c] + begin[LATE + x, c]
        return 0

    lax.fori_loop(0, 8, settle, 0)
    first = row == 0
    last = row == 7

    def column(at, held, new, brim, final):
        kinds = [[trans[at, n, 8 * t : 8 * t + 8, :] for t in range(2)] for n in range(6)]
        t_east, t_west, t_north, t_south, t_up, t_down = kinds
        for c in range(NC):
            mid = [held[at, c, 8 * t : 8 * t + 8, :] for t in range(2)]
            east = [held[at + 1, c, 8 * t : 8 * t + 8, :] for t in range(2)]
            west = [held[at - 1, c, 8 * t : 8 * t + 8, :] for t in range(2)]
            back = [pltpu.roll(tile, 7, 0) for tile in mid]
            fore = [pltpu.roll(tile, 1, 0) for tile in mid]
            north = [jnp.where(last, back[1], back[0]), jnp.where(last, back[0], back[1])]
            south = [jnp.where(first, fore[1], fore[0]), jnp.where(first, fore[0], fore[1])]
            if brim:
                outer = begin_edge[at - LATE, c] + edge[at - LATE, c]
                north[1] = jnp.where(row == 3, pltpu.roll(outer, 7, 0), north[1])
                south[1] = jnp.where(row == 4, pltpu.roll(outer, 1, 0), south[1])
            for t in range(1 if final else 2):
                value = t_east[t] * east[t] + t_west[t] * west[t]
                value = value + t_north[t] * north[t] + t_south[t] * south[t]
                value = value + t_up[t] * pltpu.roll(mid[t], 127, 1)
                value = value + t_down[t] * pltpu.roll(mid[t], 1, 1)
                part = slice(8 * t, 8 * t + 8)
                value = KEEP * mid[t] + weight[at, c, part, :] + gain[at, c, part, :] * value
                if final:
                    last_one[at - LATE, c] = value
                else:
                    new[at, c, part, :] = value

    def writing(x):
        return pltpu.make_async_copy(last_one.at[x], result.at[:, x], sems.at[x])

    def sweep(begin_at, end_at, held, new, brim=False, final=False):
        count = end_at - begin_at
        whole = count // 8 * 8

        def run(at, size):
            for step in range(size):
                column(at + step, held, new, brim, final)
                if final:
                    writing(at + step - LATE).start()
            return 0

        if whole:
            lax.fori_loop(0, whole // 8, lambda i, _: run(begin_at + i * 8, 8), 0)
        if count > whole:
            lax.fori_loop(0, 1, lambda i, _: run(begin_at + whole + i, count - whole), 0)

    sweep(1, LATE, one, two)
    sweep(LATE, LATE + 8, one, two, brim=True)
    sweep(LATE + 8, COLS - 1, one, two)
    sweep(2, COLS - 2, two, one)
    sweep(3, COLS - 3, one, two)
    sweep(4, COLS - 4, two, one)
    sweep(5, COLS - 5, one, None, final=True)
    for x in range(8):
        writing(x).wait()


def swap_pairs(shards, axis):
    axes = ("gx", "gy")
    sizes = [lax.axis_size(name) for name in axes]
    along = axes.index(axis)
    inner, outer = [], []
    for i in range(sizes[0]):
        for j in range(sizes[1]):
            place = [i, j]
            near, far_one = list(place), list(place)
            near[along] = place[along] ^ 1
            if along == 0 or 0 < place[1] < sizes[1] - 1:
                far_one[along] = (((place[along] + 1) ^ 1) - 1) % sizes[along]
            else:
                far_one[0] = i ^ 1
            here = i * sizes[1] + j
            inner.append((here, near[0] * sizes[1] + near[1]))
            outer.append((here, far_one[0] * sizes[1] + far_one[1]))
    return lax.ppermute(shards[0], axes, inner), lax.ppermute(shards[1], axes, outer)


def body(
    seg_source,
    seg_inverse,
    seg_outflow,
    well_len,
    perf_seg,
    perf_count,
    perf_coupling,
    recv_cell,
    cell_cot,
    start_iterate,
    accumulation,
    mobility,
    perm_x,
    perm_y,
    perm_z,
):
    cot = cell_cot.reshape(NC * 64, 128)
    accum = accumulation.reshape(NC * 64, 128)
    mobil = mobility.reshape(NC * 64, 128)
    held = [
        pltpu.VMEM((NC, 8, 8, 128), F32),
        pltpu.VMEM((8, 8, 128), F32),
        pltpu.VMEM((8, 8, 128), F32),
        pltpu.VMEM((8, 8, 128), F32),
        pltpu.VMEM((NC * 64, 128), BF16),
        pltpu.VMEM((NC * 64, 128), BF16),
    ]
    given = [pin(x) for x in (start_iterate, perm_x, perm_y, perm_z, accum, mobil)]
    mats, vecs, head, ratio, early_a, early_b, side_a, side_b = call(
        first_kernel,
        (
            out(81, 8, 128),
            out(NC, 8, 128),
            far(BRICKS, 8, 128),
            out(NC * 64, 128),
            far(EARLY_ROWS, 128),
            far(EARLY_ROWS, 128),
            far(SIDE_ROWS, 128),
            far(SIDE_ROWS, 128),
        ),
        [
            pltpu.VMEM((90, 8, 128), F32),
            pltpu.VMEM((BRICKS, 8, 128), F32),
            pltpu.VMEM((EARLY_ROWS, 128), F32),
            pltpu.VMEM((EARLY_ROWS, 128), F32),
            pltpu.VMEM((SIDE_ROWS, 128), F32),
            pltpu.VMEM((SIDE_ROWS, 128), F32),
            pltpu.SMEM((8,), I32),
            pltpu.VMEM((NC, 8, 128), F32),
            pltpu.VMEM((NC, NC, 8, 128), F32),
            pltpu.VMEM((NC, NC, 8, 128), F32),
        ]
        + held
        + [pltpu.SemaphoreType.DMA((10,)), pltpu.SemaphoreType.DMA((5,))],
        [HBM] * 10,
        "first",
        10_000_000,
        out_specs=(VMEM, VMEM, HBM, VMEM, HBM, HBM, HBM, HBM),
    )(pin(well_len), pin(seg_source), pin(seg_inverse), pin(seg_outflow), *given)
    heads = lax.all_to_all(head, "gy", 0, 0, tiled=True)
    early_a, early_b = swap_pairs((early_a, early_b), "gy")

    side_a, side_b = swap_pairs((side_a, side_b), "gx")
    lam, sent, token = call(
        rows_kernel,
        (
            far(NC, 8, 128),
            far(BRICKS * SLOT, 128),
            out(8, 128),
        ),
        [
            pltpu.VMEM((NC, 8, 128), F32),
            pltpu.VMEM((BRICKS * SLOT, 128), F32),
            pltpu.SMEM((BRICKS,), I32),
            pltpu.VMEM((BRICKS, 256), I32),
            pltpu.VMEM((NC, NC, BRICKS, 256), F32),
            pltpu.SemaphoreType.DMA,
            pltpu.SemaphoreType.DMA((3,)),
            pltpu.SemaphoreType.DMA((2,)),
        ],
        [HBM] * 3 + [VMEM] * 3,
        "well_rows",
        20_000_000_000,
        out_specs=(HBM, HBM, VMEM),
    )(
        pin(perf_count.reshape(BRICKS)),
        pin(perf_seg.reshape(BRICKS, 256)),
        pin(perf_coupling.reshape(NC, NC, BRICKS, 256)),
        mats,
        vecs,
        heads,
    )
    arrived = lax.all_to_all(sent, "gy", 0, 0, tiled=True)

    cell = recv_cell.reshape(BRICKS, 2, 128)
    wide, corner_a, corner_b, scale, base = call(
        shade_kernel,
        (
            far(8, FIELDS, 24, 128),
            far(CORNER_ROWS, 128),
            far(CORNER_ROWS, 128),
            far(NC * 64, 128),
            far(NC * 64, 128),
        ),
        held
        + [
            pltpu.VMEM((NC * 64, 128), BF16),
            pltpu.VMEM((8, FIELDS, 24, 128), F32),
            pltpu.VMEM((CORNER_ROWS, 128), F32),
            pltpu.VMEM((CORNER_ROWS, 128), F32),
            pltpu.VMEM((NC * 64, 128), F32),
            pltpu.VMEM((NC * 64, 128), F32),
            pltpu.SemaphoreType.DMA((7,)),
            pltpu.SemaphoreType.DMA((5,)),
        ],
        [VMEM] + [HBM] * 7 + [VMEM] * 5,
        "shade",
        limit=12,
        out_specs=(HBM,) * 5,
    )(token, *given, pin(cot), ratio, early_a, early_b, side_a, side_b)
    corner_a, corner_b = swap_pairs((corner_a, corner_b), "gx")

    weight, late_a, late_b, late_side_a, late_side_b = call(
        scatter_kernel,
        (
            out(NC * 64, 128),
            out(LATE_ROWS, 128),
            out(LATE_ROWS, 128),
            out(LATE, NC, 8, 128),
            out(LATE, NC, 8, 128),
        ),
        [
            pltpu.VMEM((576, 4096 // CHUNKS), BF16),
            pltpu.VMEM((576, 4096 // CHUNKS), BF16),
            pltpu.VMEM((256, 4096 // CHUNKS), BF16),
            pltpu.VMEM((256, 4096 // CHUNKS), BF16),
            pltpu.VMEM((NC * 64, 128), F32),
            pltpu.VMEM((NC * 64, 128), F32),
            pltpu.SemaphoreType.DMA((2,)),
        ],
        [VMEM] * 2 + [HBM] * 2,
        "scatter",
        20_000_000_000,
        limit=16,
    )(cell, arrived.reshape(BRICKS, SLOT, 128), pin(scale), pin(base))
    late_a, late_b = swap_pairs((late_a, late_b), "gy")
    late_side_a, late_side_b = swap_pairs((late_side_a, late_side_b), "gx")

    trans, gain, begin, begin_edge = call(
        early_kernel,
        (
            out(COLS, 6, 16, 128),
            out(COLS, NC, 16, 128),
            out(COLS, NC, 16, 128),
            out(8, NC, 8, 128),
        ),
        [
            pltpu.VMEM((8 + 2 * EARLY, NC, 24, 128), F32),
            pltpu.VMEM((8 + 2 * EARLY, 3, 24, 128), F32),
            pltpu.VMEM((2 * LATE, NC, 16, 128), F32),
            pltpu.VMEM((8, FIELDS, 24, 128), F32),
            pltpu.SemaphoreType.DMA,
        ],
        [HBM] + [VMEM] * 4,
        "early",
        limit=10,
    )(pin(wide), side_a, side_b, corner_a, corner_b)

    widened, edge, late_corner_a, late_corner_b = call(
        late_wide_kernel,
        (
            out(8, NC, 16, 128),
            out(8, NC, 8, 128),
            out(3, NC, 8, 128),
            out(3, NC, 8, 128),
        ),
        [],
        [VMEM] * 3,
        "late_wide",
    )(weight, late_a, late_b)
    late_corner_a, late_corner_b = swap_pairs((late_corner_a, late_corner_b), "gx")

    wide_field = pltpu.VMEM((COLS, NC, 16, 128), F32)
    result = call(
        sweep_kernel,
        out(NC, 8, 8, 128),
        [wide_field] * 3
        + [pltpu.VMEM((8, NC, 8, 128), F32), pltpu.SemaphoreType.DMA((8,))],
        [VMEM] * 10,
        "sweeps",
        out_specs=HBM,
    )(
        trans,
        gain,
        begin,
        begin_edge,
        widened,
        edge,
        late_side_a,
        late_side_b,
        late_corner_a,
        late_corner_b,
    )
    return lam, result


def solution(mesh):
    return jax.shard_map(
        body,
        mesh=mesh,
        in_specs=(
            P(None, "gx", "gy"),
            P(None, None, "gx", "gy"),
            P(None, None, "gx", "gy"),
            P("gx"),
            P("gx", "gy", None, None),
            P("gx", "gy", None),
            P(None, None, "gx", "gy", None, None),
            P("gx", "gy", None, None),
            P(None, "gx", "gy", None),
            P(None, "gx", "gy", None),
            P(None, "gx", "gy", None),
            P(None, "gx", "gy", None),
            P("gx", "gy", None),
            P("gx", "gy", None),
            P("gx", "gy", None),
        ),
        out_specs=(P(None, "gx", "gy"), P(None, "gx", "gy", None)),
        check_vma=False,
    )
```
